512 devices in a mesh: row: 16 (over y, x), col: 32 (over z, core).
Axes of the slice: x: 4, y: 4, z: 16, core: 2. Of those that a mesh axis runs over, the one named last changes fastest.
Arguments:
- tile_weights: bfloat16 [16, 32, 32, 128, 128], P('row', 'col'), may hold values from 0 to 4, as said below
- tile_pos: int32 [16, 32, 2, 32], P('row', 'col'), may hold values from 0 to 7, as said below
- tile_total: int32 [16, 32], P('row', 'col'), may hold values from 1 to 32, as said below
- root_ids: int32 [128], replicated, may hold values from 0 to 16383
Outputs:
- hop_level: int32 [16384, 128], P(('row', 'col'))
- path_share: float32 [16384, 128], P(('row', 'col'))
- found_per_level: float32 [4, 128], replicated
The draws below stay inside these ranges and needn't reach their ends.
Inputs may be any that keep to these rules, and one draw needn't show every extreme that they name: `tile_weights`: nonnegative; an entry is zero wherever the tile has no edge. `tile_pos`: the slots of one device name distinct tile positions; tile rows lie below 8 and tile columns below 4. `tile_total`: some device uses all 32 slots; slots at or past a device's total hold arbitrary positions and zero weights.
All inputs are finite; a program needn't handle non-finite values.
Results may differ from the reference program's by a relative error of at most 0.01.
Values may be sent and summed in bfloat16 or wider, within the bound.
No kernel may reach another device: no remote copies, remote signals or barrier semaphores. Data moves between devices by JAX's collectives and lax.ppermute only.
A program may use at most 64 MiB of HBM per device.

```python
import jax
import jax.numpy as jnp
from jax import lax

ROOTS = 128
PV = 32
LEVELS = 4
VERTICES = 16384
ROW_BLOCK = 1024
COL_BLOCK = 512
TILES_DEV = 32
N_ROW = 16
N_COL = 32


def graph_layout(key):
    base = jax.random.fold_in(key, 5)
    device_count = N_ROW * N_COL
    bit_count = (VERTICES - 1).bit_length()
    edge_count = 16 * VERTICES
    dest_ids = jnp.zeros((edge_count,), jnp.int32)
    source_ids = jnp.zeros((edge_count,), jnp.int32)
    for bit_level in range(bit_count):
        pick = jax.random.randint(jax.random.fold_in(base, bit_level), (edge_count,), 0, 100, jnp.int32)
        down_bit = (pick >= 76).astype(jnp.int32)
        right_bit = ((pick >= 57) & (pick < 76) | (pick >= 95)).astype(jnp.int32)
        dest_ids = dest_ids * 2 + down_bit
        source_ids = source_ids * 2 + right_bit
    dest_ids = dest_ids % VERTICES
    source_ids = source_ids % VERTICES
    row_tiles = ROW_BLOCK // 128
    col_tiles = COL_BLOCK // 128
    positions = row_tiles * col_tiles
    block_row = dest_ids // ROW_BLOCK
    inner_row = dest_ids % ROW_BLOCK
    block_col = source_ids // PV % N_COL
    inner_col = source_ids // (PV * N_COL) * PV + source_ids % PV
    device_ids = block_row * N_COL + block_col
    tile_ids = device_ids * positions + inner_row // 128 * col_tiles + inner_col // 128
    hits = jnp.zeros((device_count * positions,), jnp.int32).at[tile_ids].add(1)
    hits = jnp.minimum(hits, 1 << 20).reshape(device_count, positions)
    order_keys = jax.random.split(jax.random.fold_in(base, 997), device_count)
    ranks = jax.vmap(lambda one_key: jax.random.permutation(one_key, positions).astype(jnp.int32))(order_keys)
    scores = hits * positions + ranks
    _, chosen = lax.top_k(scores, TILES_DEV)
    chosen = chosen.astype(jnp.int32)
    slot_keys = jax.random.split(jax.random.fold_in(base, 1999), device_count)
    slot_order = jax.vmap(lambda one_key: jax.random.permutation(one_key, TILES_DEV).astype(jnp.int32))(slot_keys)
    chosen = jnp.take_along_axis(chosen, slot_order, axis=1)
    totals = jax.random.randint(jax.random.fold_in(base, 2999), (device_count,), 1, TILES_DEV + 1, jnp.int32)
    fullest = jax.random.randint(jax.random.fold_in(base, 3999), (), 0, device_count, jnp.int32)
    totals = totals.at[fullest].set(TILES_DEV)
    slot_index = jnp.broadcast_to(jnp.arange(TILES_DEV, dtype=jnp.int32)[None, :], (device_count, TILES_DEV))
    flat_chosen = (jnp.arange(device_count, dtype=jnp.int32)[:, None] * positions + chosen).reshape(-1)
    slot_of = jnp.full((device_count * positions,), -1, jnp.int32).at[flat_chosen].set(slot_index.reshape(-1))
    edge_slot = slot_of[tile_ids]
    keep = (edge_slot >= 0) & (edge_slot < totals[device_ids])
    cell = (device_ids * TILES_DEV + jnp.maximum(edge_slot, 0)) * 16384 + inner_row % 128 * 128 + inner_col % 128
    cell = jnp.where(keep, cell, device_count * TILES_DEV * 16384)
    return (chosen, totals, cell, edge_count)


def draw_tile_weights(key, part):
    chosen, totals, cell, edge_count = graph_layout(key)
    value_key = jax.random.fold_in(key, 77)
    values = jnp.exp(jax.random.uniform(value_key, (edge_count,), jnp.float32, jnp.log(0.5), jnp.log(2.0)))
    flat = jnp.zeros((N_ROW * N_COL * TILES_DEV * 16384,), jnp.bfloat16)
    flat = flat.at[cell].max(values.astype(jnp.bfloat16), mode='drop')
    return flat.reshape(N_ROW, N_COL, TILES_DEV, 128, 128)


def draw_tile_pos(key, part):
    chosen, totals, cell, edge_count = graph_layout(key)
    col_tiles = COL_BLOCK // 128
    stacked = jnp.stack([chosen // col_tiles, chosen % col_tiles], axis=1)
    return stacked.reshape(N_ROW, N_COL, 2, TILES_DEV).astype(jnp.int32)


def draw_tile_total(key, part):
    chosen, totals, cell, edge_count = graph_layout(key)
    return totals.reshape(N_ROW, N_COL).astype(jnp.int32)


def touch_ends(values, rng, low, high):
    longest = values.shape.index(max(values.shape))
    spots = []
    for shift in (0, 1):
        where = [jax.random.randint(jax.random.fold_in(rng, axis), (), 0, length) for axis, length in enumerate(values.shape)]
        where[longest] = (where[longest] + shift) % values.shape[longest]
        spots.append(tuple(where))
    return values.at[spots[0]].set(low).at[spots[1]].set(high)


def setup_inputs(seed: int = 0) -> dict:
    arg_keys = jax.random.split(jax.random.key(seed), 5)
    tile_weights = draw_tile_weights(jax.random.fold_in(arg_keys[4], 71), 0)
    tile_pos = draw_tile_pos(jax.random.fold_in(arg_keys[4], 71), 0)
    tile_total = draw_tile_total(jax.random.fold_in(arg_keys[4], 71), 0)
    root_ids = touch_ends(jax.random.randint(arg_keys[3], (ROOTS,), 0, VERTICES), jax.random.fold_in(arg_keys[3], 1), 0, VERTICES - 1).astype(jnp.int32)
    return {"tile_weights": tile_weights, "tile_pos": tile_pos, "tile_total": tile_total, "root_ids": root_ids}


def device_partial(frontier, tiles, dest_tiles, source_tiles, limit, col_index):
    offsets = jnp.arange(128, dtype=jnp.int32)

    def advance(total, slot):
        tile = tiles[slot].astype(jnp.float32)
        local_cols = source_tiles[slot] * 128 + offsets
        global_cols = ((local_cols // PV) * N_COL + col_index) * PV + local_cols % PV
        block = frontier[global_cols].astype(jnp.float32)
        contrib = jnp.dot(tile, block, precision=lax.Precision.HIGHEST)
        contrib = contrib * (slot < limit).astype(jnp.float32)
        start = (dest_tiles[slot] * 128).astype(jnp.int32)
        current = lax.dynamic_slice_in_dim(total, start, 128, 0)
        return lax.dynamic_update_slice_in_dim(total, current + contrib, start, 0), None

    total = jnp.zeros((PV * N_COL, ROOTS), jnp.float32)
    total, _ = lax.scan(advance, total, jnp.arange(TILES_DEV, dtype=jnp.int32))
    return total


def propagate(frontier, dev_tiles, dev_dest, dev_source, dev_total):
    row_block = PV * N_COL
    arrived = jnp.zeros((PV * N_ROW * N_COL, ROOTS), jnp.float32)

    def each_device(carry, device):
        row_index = device // N_COL
        col_index = device % N_COL
        partial_value = device_partial(frontier, dev_tiles[device], dev_dest[device], dev_source[device], dev_total[device], col_index)
        rounded = lax.optimization_barrier(partial_value.astype(jnp.bfloat16)).astype(jnp.float32)
        start = (row_index * row_block).astype(jnp.int32)
        current = lax.dynamic_slice_in_dim(carry, start, row_block, 0)
        return lax.dynamic_update_slice_in_dim(carry, current + rounded, start, 0), None

    arrived, _ = lax.scan(each_device, arrived, jnp.arange(N_ROW * N_COL, dtype=jnp.int32))
    return arrived


def reference(tile_weights, tile_pos, tile_total, root_ids):
    device_count = N_ROW * N_COL
    dev_tiles = tile_weights.reshape(device_count, TILES_DEV, 128, 128)
    dev_dest = tile_pos[:, :, 0, :].reshape(device_count, TILES_DEV).astype(jnp.int32)
    dev_source = tile_pos[:, :, 1, :].reshape(device_count, TILES_DEV).astype(jnp.int32)
    dev_total = tile_total.reshape(device_count).astype(jnp.int32)
    vertex_ids = jnp.arange(PV * N_ROW * N_COL, dtype=jnp.int32)
    is_root = vertex_ids[:, None] == root_ids[None, :]
    path_now = is_root.astype(jnp.float32)
    kept_weight = path_now
    hop_level = jnp.where(is_root, 0, LEVELS + 1).astype(jnp.int32)
    found_counts = []
    found_totals = []
    for level_num in range(LEVELS):
        frontier = path_now.astype(jnp.bfloat16)
        arrived = propagate(frontier, dev_tiles, dev_dest, dev_source, dev_total)
        newly = (arrived > 0) & (hop_level == LEVELS + 1)
        path_now = jnp.where(newly, arrived, jnp.float32(0.0))
        hop_level = jnp.where(newly, jnp.int32(level_num + 1), hop_level)
        kept_weight = kept_weight + path_now
        found_counts.append(jnp.sum(newly.astype(jnp.float32), axis=0))
        found_totals.append(jnp.sum(path_now, axis=0))
    counts = jnp.stack(found_counts)
    totals = jnp.stack(found_totals)
    factor = counts / jnp.maximum(totals, 1.0)
    factor_table = jnp.concatenate([jnp.ones((1, ROOTS), jnp.float32), factor, jnp.zeros((1, ROOTS), jnp.float32)], axis=0)
    scale = jnp.zeros_like(kept_weight)
    for level_num in range(LEVELS + 2):
        scale = scale + jnp.where(hop_level == level_num, factor_table[level_num][None, :], jnp.float32(0.0))
    return hop_level, kept_weight * scale, counts
```

```python
import jax
import jax.numpy as jnp
from jax import lax
from jax.experimental import pallas as pl
from jax.experimental.pallas import tpu as pltpu
from jax.sharding import Mesh
from jax.sharding import PartitionSpec as P

ROOTS = 128
HALF = ROOTS // 2
PV = 32
LEVELS = 4
TILE = 128
Y, X, Z, C = "y", "x", "z", "c"
ROW = (Y, X)
COL = (Z, C)
VMEM = pl.BlockSpec(memory_space=pltpu.VMEM)
SMEM = pl.BlockSpec(memory_space=pltpu.SMEM)
BF = jnp.bfloat16
F32 = jnp.float32


def build_kernel(pos_ref, total_ref, core_ref, tiles_ref, dense_ref):
    columns = dense_ref.shape[1] // 2
    core = core_ref[0]
    dense_ref[...] = jnp.zeros_like(dense_ref)

    def place(slot, carry):
        dest, source = pos_ref[0, slot], pos_ref[1, slot]
        for part in range(2):
            for half in range(2):
                first = pl.multiple_of(part * 2 * PV + (half ^ core) * PV, PV)
                rows = pl.multiple_of(dest * 2 * PV + part * PV, PV)
                lanes = pl.multiple_of(half * columns + source * TILE, TILE)
                dense_ref[pl.ds(rows, PV), pl.ds(lanes, TILE)] = tiles_ref[slot, pl.ds(first, PV), :]
        return carry

    lax.fori_loop(0, total_ref[0], place, 0)


def products(own_ref, other_ref, front, turned, sent_ref):
    rows = front.shape[0]
    left = lax.broadcasted_iota(jnp.int32, front.shape, 1) < HALF
    zero = jnp.zeros_like(front)

    def times(ref, half, value):
        return jnp.dot(
            ref[:, half * rows : (half + 1) * rows], value.astype(BF), preferred_element_type=F32
        )

    total = times(own_ref, 0, jnp.where(left, front, zero))
    total += times(own_ref, 1, jnp.where(left, zero, turned))
    total += times(other_ref, 0, jnp.where(left, zero, front))
    total += times(other_ref, 1, jnp.where(left, turned, zero))
    sent_ref[...] = total.astype(BF)


def first_kernel(base_ref, roots_ref, own_ref, other_ref, sent_ref):
    shape = sent_ref.shape
    row = lax.broadcasted_iota(jnp.int32, shape, 0)
    left = lax.broadcasted_iota(jnp.int32, shape, 1) < HALF
    vertex = (row // PV) * base_ref[2] + row % PV
    roots = roots_ref[...]
    front = (vertex + jnp.where(left, base_ref[0], base_ref[1]) == roots).astype(F32)
    turned = (vertex + jnp.where(left, base_ref[1], base_ref[0]) == roots).astype(F32)
    products(own_ref, other_ref, front, turned, sent_ref)


def level_kernel(front_ref, own_ref, other_ref, sent_ref):
    front = front_ref[...].astype(F32)
    products(own_ref, other_ref, front, pltpu.roll(front, HALF, 1), sent_ref)


def to_peers(value, axis):
    peers = lax.axis_size(axis)
    return lax.all_to_all(jnp.broadcast_to(value[None], (peers, *value.shape)), axis, 0, 0, tiled=True)


def local(tile_weights, tile_pos, tile_total, root_ids):
    rows_all, z_all = lax.axis_size(ROW), lax.axis_size(Z)
    row_index, z_index, core = lax.axis_index(ROW), lax.axis_index(Z), lax.axis_index(C)
    row_block = z_all * 2 * PV
    sources = rows_all * PV
    dests = z_all * PV
    own = pl.pallas_call(
        build_kernel,
        out_shape=jax.ShapeDtypeStruct((dests, 2 * sources), BF),
        in_specs=[SMEM, SMEM, SMEM, VMEM],
        out_specs=VMEM,
    )(tile_pos[0, 0], tile_total[0], core[None].astype(jnp.int32), tile_weights[0, 0])
    other = lax.ppermute(own, C, [(0, 1), (1, 0)])

    my_roots = lax.dynamic_slice_in_dim(root_ids, core * HALF, HALF)
    my_roots = jnp.concatenate([my_roots, my_roots])[None]
    base_own = z_index * 2 * PV + core * PV
    base_other = z_index * 2 * PV + (1 - core) * PV
    bases = jnp.stack([base_own, base_other, jnp.int32(row_block)]).astype(jnp.int32)
    offset = jnp.where(jnp.arange(ROOTS) < HALF, base_own, base_other)[None]
    vertex = row_index * row_block + jnp.arange(PV, dtype=jnp.int32)[:, None] + offset
    is_root = vertex == my_roots
    kept = is_root.astype(F32)
    hop = jnp.where(is_root, 0, LEVELS + 1).astype(jnp.int32)

    product_shape = jax.ShapeDtypeStruct((dests, ROOTS), BF)
    counts, totals = [], []
    front = None
    for level in range(1, LEVELS + 1):
        if level == 1:
            sent = pl.pallas_call(
                first_kernel, out_shape=product_shape, in_specs=[SMEM, VMEM, VMEM, VMEM], out_specs=VMEM
            )(bases, my_roots, own, other)
        else:
            front = to_peers(front, ROW).reshape(sources, ROOTS)
            sent = pl.pallas_call(
                level_kernel, out_shape=product_shape, in_specs=[VMEM] * 3, out_specs=VMEM
            )(front, own, other)
        arrived = lax.all_to_all(sent.reshape(z_all, PV, ROOTS), Z, 0, 0, tiled=True)
        arrived = arrived.astype(F32).sum(axis=0)
        newly = (arrived > 0) & (hop == LEVELS + 1)
        path = jnp.where(newly, arrived, 0.0)
        hop = jnp.where(newly, level, hop)
        kept = kept + path
        front = path.astype(BF)
        counts.append(newly.astype(F32).sum(axis=0))
        totals.append(path.sum(axis=0))

    theirs = jnp.concatenate([hop[:, HALF:].astype(F32), kept[:, HALF:]], axis=1)
    theirs = lax.ppermute(theirs, C, [(0, 1), (1, 0)])

    counts, totals = jnp.stack(counts), jnp.stack(totals)
    sums = jnp.concatenate(
        [counts[:, :HALF] + counts[:, HALF:], totals[:, :HALF] + totals[:, HALF:]], axis=1
    )
    sums = to_peers(sums, (Y, X, C)).reshape(rows_all, 2 * LEVELS, ROOTS).sum(axis=0)
    sums = to_peers(sums, Z).sum(axis=0).reshape(2, LEVELS, ROOTS)
    counts = jnp.concatenate([sums[0, :, :HALF], sums[1, :, :HALF]], axis=1)
    totals = jnp.concatenate([sums[0, :, HALF:], sums[1, :, HALF:]], axis=1)

    def joined(mine, received):
        return jnp.where(
            core == 0,
            jnp.concatenate([mine, received], axis=1),
            jnp.concatenate([received, mine], axis=1),
        )

    hop = joined(hop[:, :HALF], theirs[:, :HALF].astype(jnp.int32))
    kept = joined(kept[:, :HALF], theirs[:, HALF:])
    factor = counts / jnp.maximum(totals, 1.0)
    scale = jnp.where(hop == 0, 1.0, 0.0)
    for level in range(1, LEVELS + 1):
        scale = scale + jnp.where(hop == level, factor[level - 1][None], 0.0)
    return hop, kept * scale, counts


def solution(mesh):
    torus = Mesh(mesh.devices.reshape(4, 4, 16, 2), (Y, X, Z, C))
    return jax.shard_map(
        local,
        mesh=torus,
        in_specs=(P(ROW, COL, None, None, None), P(ROW, COL, None, None), P(ROW, COL), P()),
        out_specs=(P((Y, X, Z, C), None), P((Y, X, Z, C), None), P()),
        check_vma=False,
    )
```

```python
import functools

import jax
import jax.numpy as jnp
from jax import lax
from jax.experimental import pallas as pl
from jax.experimental.pallas import tpu as pltpu
from jax.sharding import Mesh
from jax.sharding import PartitionSpec as P

ROOTS = 128
HALF = ROOTS // 2
PV = 32
LEVELS = 4
TILE = 128
GRANT = 8 << 20
Y, X, Z, C = "y", "x", "z", "c"
ROW = (Y, X)
COL = (Z, C)
VMEM = pl.BlockSpec(memory_space=pltpu.VMEM)
SMEM = pl.BlockSpec(memory_space=pltpu.SMEM)
BF = jnp.bfloat16
F32 = jnp.float32


def call(kernel, out_shape, in_specs, *operands):
    return pl.pallas_call(
        kernel,
        out_shape=out_shape,
        in_specs=in_specs,
        out_specs=jax.tree.map(lambda _: VMEM, out_shape),
        compiler_params=pltpu.CompilerParams(vmem_limit_bytes=GRANT),
    )(*operands)


def build_kernel(pos_ref, total_ref, tiles_ref, dense_ref):
    columns = dense_ref.shape[1] // 2
    core = lax.axis_index(C)
    dense_ref[...] = jnp.zeros_like(dense_ref)

    def place(slot, carry):
        dest, source = pos_ref[0, slot], pos_ref[1, slot]
        for part in range(2):
            for half in range(2):
                first = pl.multiple_of(part * 2 * PV + (half ^ core) * PV, PV)
                rows = pl.multiple_of(dest * 2 * PV + part * PV, PV)
                lanes = pl.multiple_of(half * columns + source * TILE, TILE)
                dense_ref[pl.ds(rows, PV), pl.ds(lanes, TILE)] = tiles_ref[slot, pl.ds(first, PV), :]
        return carry

    lax.fori_loop(0, total_ref[0, 0], place, 0)


def left_half(shape):
    return lax.broadcasted_iota(jnp.int32, shape, len(shape) - 1) < HALF


def own_roots(roots_ref):
    roots = roots_ref[...]
    turned = pltpu.roll(roots, HALF, 1)
    return jnp.where(left_half(roots.shape) == (lax.axis_index(C) == 0), roots, turned)


def products(own_ref, other_ref, front, turned, sent_ref):
    rows = front.shape[0]
    left = left_half(front.shape)
    zero = jnp.zeros_like(front)

    def times(ref, half, value):
        return jnp.dot(
            ref[:, half * rows : (half + 1) * rows], value.astype(BF), preferred_element_type=F32
        )

    total = times(own_ref, 0, jnp.where(left, front, zero))
    total += times(own_ref, 1, jnp.where(left, zero, turned))
    total += times(other_ref, 0, jnp.where(left, zero, front))
    total += times(other_ref, 1, jnp.where(left, turned, zero))
    sent_ref[...] = total.astype(BF)


def first_kernel(row_block, roots_ref, own_ref, other_ref, sent_ref, hop_ref, kept_ref):
    core, pair = lax.axis_index(C), lax.axis_index(Z) * 2 * PV
    base_own, base_other = pair + core * PV, pair + (1 - core) * PV
    roots = own_roots(roots_ref)
    shape = (own_ref.shape[1] // 2, ROOTS)
    row = lax.broadcasted_iota(jnp.int32, shape, 0)
    left = left_half(shape)
    vertex = (row // PV) * row_block + row % PV
    front = (vertex + jnp.where(left, base_own, base_other) == roots).astype(F32)
    turned = (vertex + jnp.where(left, base_other, base_own) == roots).astype(F32)
    products(own_ref, other_ref, front, turned, sent_ref)
    state = hop_ref.shape
    vertex = lax.broadcasted_iota(jnp.int32, state, 0) + lax.axis_index(ROW) * row_block
    is_root = vertex + jnp.where(left_half(state), base_own, base_other) == roots
    kept_ref[...] = is_root.astype(F32)
    hop_ref[...] = jnp.where(is_root, 0, LEVELS + 1)


def level_kernel(front_ref, own_ref, other_ref, sent_ref):
    front = front_ref[...].astype(F32)
    products(own_ref, other_ref, front, pltpu.roll(front, HALF, 1), sent_ref)


def found(level, parts_ref, hop_ref, kept_ref):
    arrived = parts_ref[0].astype(F32)
    for peer in range(1, parts_ref.shape[0]):
        arrived += parts_ref[peer].astype(F32)
    hop = hop_ref[...]
    newly = (arrived > 0) & (hop == LEVELS + 1)
    path = jnp.where(newly, arrived, 0.0)
    return jnp.where(newly, level, hop), kept_ref[...] + path, path


def update_kernel(level, parts_ref, hop_in, kept_in, hop_ref, kept_ref, front_ref):
    hop_ref[...], kept_ref[...], path = found(level, parts_ref, hop_in, kept_in)
    path = path.astype(BF)
    for peer in range(front_ref.shape[0]):
        front_ref[peer] = path


def last_kernel(parts_ref, hop_in, kept_in, mine_ref, theirs_ref, sums_ref):
    hop, kept, _ = found(LEVELS, parts_ref, hop_in, kept_in)
    hops = hop.astype(F32)
    left = left_half(hop.shape)
    mine_ref[...] = jnp.where(left, hops, pltpu.roll(kept, HALF, 1))
    theirs_ref[...] = jnp.where(left, pltpu.roll(hops, HALF, 1), kept)
    sums = []
    for level in range(1, LEVELS + 1):
        at = hop == level
        count = jnp.sum(at.astype(F32), axis=0, keepdims=True)
        total = jnp.sum(jnp.where(at, kept, 0.0), axis=0, keepdims=True)
        count, total = count + pltpu.roll(count, HALF, 1), total + pltpu.roll(total, HALF, 1)
        sums.append(jnp.where(left_half(count.shape), count, total))
    sums = jnp.concatenate(sums, axis=0)
    for peer in range(sums_ref.shape[0]):
        sums_ref[peer] = sums


def sum_kernel(parts_ref, sums_ref):
    sums = jnp.sum(parts_ref[...], axis=0)
    for peer in range(sums_ref.shape[0]):
        sums_ref[peer] = sums


def end_kernel(sums_ref, mine_ref, theirs_ref, hop_ref, share_ref, counts_ref):
    parts = sums_ref[...]
    sums = jnp.sum(parts.reshape(parts.shape[0] // 2, 2, *parts.shape[1:]), axis=0)
    first, second = sums[0], sums[1]
    left = left_half(first.shape)
    counts = jnp.where(left, first, pltpu.roll(second, HALF, 1))
    totals = jnp.where(left, pltpu.roll(first, HALF, 1), second)
    counts_ref[...] = counts
    factor = counts / jnp.maximum(totals, 1.0)
    mine, theirs = mine_ref[...], theirs_ref[...]
    is_first = lax.axis_index(C) == 0
    low, high = jnp.where(is_first, mine, theirs), jnp.where(is_first, theirs, mine)
    left = left_half(low.shape)
    hop = jnp.where(left, low, pltpu.roll(high, HALF, 1)).astype(jnp.int32)
    kept = jnp.where(left, pltpu.roll(low, HALF, 1), high)
    scale = jnp.where(hop == 0, 1.0, 0.0)
    for level in range(1, LEVELS + 1):
        scale = jnp.where(hop == level, factor[level - 1 : level], scale)
    hop_ref[...] = hop
    share_ref[...] = kept * scale


def exchanged(value, axis):
    return lax.all_to_all(value, axis, 0, 0, tiled=True)


def local(tile_weights, tile_pos, tile_total, root_ids):
    rows_all, z_all = lax.axis_size(ROW), lax.axis_size(Z)
    row_block, sources, dests = z_all * 2 * PV, rows_all * PV, z_all * PV
    bf = lambda *shape: jax.ShapeDtypeStruct(shape, BF)
    f32 = lambda *shape: jax.ShapeDtypeStruct(shape, F32)
    hops = jax.ShapeDtypeStruct((PV, ROOTS), jnp.int32)
    swap = [(0, 1), (1, 0)]

    own = call(build_kernel, bf(dests, 2 * sources), [SMEM, SMEM, VMEM], tile_pos[0, 0], tile_total, tile_weights[0, 0])
    other = lax.ppermute(own, C, swap)
    sent, hop, kept = call(
        functools.partial(first_kernel, row_block),
        (bf(dests, ROOTS), hops, f32(PV, ROOTS)),
        [VMEM] * 3,
        root_ids[None],
        own,
        other,
    )
    for level in range(1, LEVELS):
        parts = exchanged(sent.reshape(z_all, PV, ROOTS), Z)
        hop, kept, front = call(
            functools.partial(update_kernel, level),
            (hops, f32(PV, ROOTS), bf(rows_all, PV, ROOTS)),
            [VMEM] * 3,
            parts,
            hop,
            kept,
        )
        front = exchanged(front, ROW).reshape(sources, ROOTS)
        sent = call(level_kernel, bf(dests, ROOTS), [VMEM] * 3, front, own, other)
    parts = exchanged(sent.reshape(z_all, PV, ROOTS), Z)
    mine, theirs, sums = call(
        last_kernel,
        (f32(PV, ROOTS), f32(PV, ROOTS), f32(z_all, LEVELS, ROOTS)),
        [VMEM] * 3,
        parts,
        hop,
        kept,
    )
    theirs = lax.ppermute(theirs, C, swap)
    sums = exchanged(sums, Z)
    sums = call(sum_kernel, f32(2 * rows_all, LEVELS, ROOTS), [VMEM], sums)
    sums = exchanged(sums, (Y, X, C))
    return call(end_kernel, (hops, f32(PV, ROOTS), f32(LEVELS, ROOTS)), [VMEM] * 3, sums, mine, theirs)


def solution(mesh):
    torus = Mesh(mesh.devices.reshape(4, 4, 16, 2), (Y, X, Z, C))
    return jax.shard_map(
        local,
        mesh=torus,
        in_specs=(P(ROW, COL, None, None, None), P(ROW, COL, None, None), P(ROW, COL), P()),
        out_specs=(P((Y, X, Z, C), None), P((Y, X, Z, C), None), P()),
        check_vma=False,
    )
```

```python
import functools

import jax
import jax.numpy as jnp
from jax import lax
from jax.experimental import pallas as pl
from jax.experimental.pallas import tpu as pltpu
from jax.sharding import Mesh
from jax.sharding import PartitionSpec as P

ROOTS = 128
HALF = ROOTS // 2
PV = 32
LEVELS = 4
TILE = 128
GRANT = 8 << 20
BUILD_GRANT = 209 << 18
CHUNKS = 4
Y, X, Z, C = "y", "x", "z", "c"
ROW = (Y, X)
COL = (Z, C)
VMEM = pl.BlockSpec(memory_space=pltpu.VMEM)
SMEM = pl.BlockSpec(memory_space=pltpu.SMEM)
ANY = pl.BlockSpec(memory_space=pl.ANY)
BF = jnp.bfloat16
F32 = jnp.float32


def call(kernel, out_shape, in_specs, *operands, scratch=(), grant=GRANT):
    return pl.pallas_call(
        kernel,
        out_shape=out_shape,
        in_specs=in_specs,
        out_specs=jax.tree.map(lambda _: VMEM, out_shape),
        scratch_shapes=scratch,
        compiler_params=pltpu.CompilerParams(vmem_limit_bytes=grant),
    )(*operands)


def build_kernel(total_ref, pos_ref, tiles_any, dense_ref, tiles_ref, tile_sems):
    columns = dense_ref.shape[1] // 2
    core = lax.axis_index(C)
    slots = tiles_ref.shape[0]
    step = slots // CHUNKS
    tile_copies = []
    for chunk in range(CHUNKS):
        part = pl.ds(chunk * step, step)
        tile_copies.append(pltpu.make_async_copy(tiles_any.at[part], tiles_ref.at[part], tile_sems.at[chunk]))
        tile_copies[-1].start()
    dense_ref[...] = jnp.zeros_like(dense_ref)

    def place(slot, carry):
        dest, source = pos_ref[0, slot], pos_ref[1, slot]
        for part in range(2):
            for half in range(2):
                first = pl.multiple_of(part * 2 * PV + (half ^ core) * PV, PV)
                rows = pl.multiple_of(dest * 2 * PV + part * PV, PV)
                lanes = pl.multiple_of(half * columns + source * TILE, TILE)
                dense_ref[pl.ds(rows, PV), pl.ds(lanes, TILE)] = tiles_ref[slot, pl.ds(first, PV), :]
        return carry

    for chunk in range(CHUNKS):
        tile_copies[chunk].wait()
        lax.fori_loop(chunk * step, jnp.minimum(total_ref[0, 0], (chunk + 1) * step), place, 0)


def left_half(shape):
    return lax.broadcasted_iota(jnp.int32, shape, len(shape) - 1) < HALF


def own_roots(roots_ref):
    roots = roots_ref[...]
    turned = pltpu.roll(roots, HALF, 1)
    return jnp.where(left_half(roots.shape) == (lax.axis_index(C) == 0), roots, turned)


def times(ref, half, value):
    rows = value.shape[0]
    return jnp.dot(ref[:, half * rows : (half + 1) * rows], value.astype(BF), preferred_element_type=F32)


def own_products(own_ref, front, turned):
    left = left_half(front.shape)
    zero = jnp.zeros_like(front)
    return times(own_ref, 0, jnp.where(left, front, zero)) + times(own_ref, 1, jnp.where(left, zero, turned))


def other_products(other_ref, front, turned):
    left = left_half(front.shape)
    zero = jnp.zeros_like(front)
    return times(other_ref, 0, jnp.where(left, zero, front)) + times(other_ref, 1, jnp.where(left, turned, zero))


def root_front(row_block, roots_ref, sources):
    core, pair = lax.axis_index(C), lax.axis_index(Z) * 2 * PV
    base_own, base_other = pair + core * PV, pair + (1 - core) * PV
    roots = own_roots(roots_ref)
    shape = (sources, ROOTS)
    row = lax.broadcasted_iota(jnp.int32, shape, 0)
    left = left_half(shape)
    vertex = (row // PV) * row_block + row % PV
    front = (vertex + jnp.where(left, base_own, base_other) == roots).astype(F32)
    turned = (vertex + jnp.where(left, base_other, base_own) == roots).astype(F32)
    return front, turned


def first_own_kernel(row_block, roots_ref, own_ref, part_ref, hop_ref, kept_ref):
    front, turned = root_front(row_block, roots_ref, own_ref.shape[1] // 2)
    part_ref[...] = own_products(own_ref, front, turned)
    core, pair = lax.axis_index(C), lax.axis_index(Z) * 2 * PV
    base_own, base_other = pair + core * PV, pair + (1 - core) * PV
    state = hop_ref.shape
    vertex = lax.broadcasted_iota(jnp.int32, state, 0) + lax.axis_index(ROW) * row_block
    is_root = vertex + jnp.where(left_half(state), base_own, base_other) == own_roots(roots_ref)
    kept_ref[...] = is_root.astype(F32)
    hop_ref[...] = jnp.where(is_root, 0, LEVELS + 1)


def first_other_kernel(row_block, roots_ref, other_ref, part_ref, sent_ref):
    front, turned = root_front(row_block, roots_ref, other_ref.shape[1] // 2)
    sent_ref[...] = (part_ref[...] + other_products(other_ref, front, turned)).astype(BF)


def level_kernel(front_ref, own_ref, other_ref, sent_ref):
    front = front_ref[...].astype(F32)
    turned = pltpu.roll(front, HALF, 1)
    total = own_products(own_ref, front, turned) + other_products(other_ref, front, turned)
    sent_ref[...] = total.astype(BF)


def found(level, parts_ref, hop_ref, kept_ref):
    arrived = parts_ref[0].astype(F32)
    for peer in range(1, parts_ref.shape[0]):
        arrived += parts_ref[peer].astype(F32)
    hop = hop_ref[...]
    newly = (arrived > 0) & (hop == LEVELS + 1)
    path = jnp.where(newly, arrived, 0.0)
    return jnp.where(newly, level, hop), kept_ref[...] + path, path


def update_kernel(level, parts_ref, hop_in, kept_in, hop_ref, kept_ref, front_ref):
    hop_ref[...], kept_ref[...], path = found(level, parts_ref, hop_in, kept_in)
    path = path.astype(BF)
    for peer in range(front_ref.shape[0]):
        front_ref[peer] = path


def last_kernel(parts_ref, hop_in, kept_in, mine_ref, theirs_ref, sums_ref):
    hop, kept, _ = found(LEVELS, parts_ref, hop_in, kept_in)
    hops = hop.astype(F32)
    left = left_half(hop.shape)
    mine_ref[...] = jnp.where(left, hops, pltpu.roll(kept, HALF, 1))
    theirs_ref[...] = jnp.where(left, pltpu.roll(hops, HALF, 1), kept)
    sums = []
    for level in range(1, LEVELS + 1):
        at = hop == level
        count = jnp.sum(at.astype(F32), axis=0, keepdims=True)
        total = jnp.sum(jnp.where(at, kept, 0.0), axis=0, keepdims=True)
        count, total = count + pltpu.roll(count, HALF, 1), total + pltpu.roll(total, HALF, 1)
        sums.append(jnp.where(left_half(count.shape), count, total))
    sums = jnp.concatenate(sums, axis=0)
    for peer in range(sums_ref.shape[0]):
        sums_ref[peer] = sums


def sum_kernel(parts_ref, sums_ref):
    sums = jnp.sum(parts_ref[...], axis=0)
    for peer in range(sums_ref.shape[0]):
        sums_ref[peer] = sums


def end_kernel(sums_ref, mine_ref, theirs_ref, hop_ref, share_ref, counts_ref):
    parts = sums_ref[...]
    sums = jnp.sum(parts.reshape(parts.shape[0] // 2, 2, *parts.shape[1:]), axis=0)
    first, second = sums[0], sums[1]
    left = left_half(first.shape)
    counts = jnp.where(left, first, pltpu.roll(second, HALF, 1))
    totals = jnp.where(left, pltpu.roll(first, HALF, 1), second)
    counts_ref[...] = counts
    factor = counts / jnp.maximum(totals, 1.0)
    mine, theirs = mine_ref[...], theirs_ref[...]
    is_first = lax.axis_index(C) == 0
    low, high = jnp.where(is_first, mine, theirs), jnp.where(is_first, theirs, mine)
    left = left_half(low.shape)
    hop = jnp.where(left, low, pltpu.roll(high, HALF, 1)).astype(jnp.int32)
    kept = jnp.where(left, pltpu.roll(low, HALF, 1), high)
    scale = jnp.where(hop == 0, 1.0, 0.0)
    for level in range(1, LEVELS + 1):
        scale = jnp.where(hop == level, factor[level - 1 : level], scale)
    hop_ref[...] = hop
    share_ref[...] = kept * scale


def exchanged(value, axis):
    return lax.all_to_all(value, axis, 0, 0, tiled=True)


def local(tile_weights, tile_pos, tile_total, root_ids):
    rows_all, z_all = lax.axis_size(ROW), lax.axis_size(Z)
    row_block, sources, dests = z_all * 2 * PV, rows_all * PV, z_all * PV
    bf = lambda *shape: jax.ShapeDtypeStruct(shape, BF)
    f32 = lambda *shape: jax.ShapeDtypeStruct(shape, F32)
    hops = jax.ShapeDtypeStruct((PV, ROOTS), jnp.int32)
    swap = [(0, 1), (1, 0)]

    slots = tile_weights.shape[2]
    own = call(
        build_kernel,
        bf(dests, 2 * sources),
        [SMEM, SMEM, ANY],
        tile_total,
        tile_pos[0, 0],
        tile_weights[0, 0],
        grant=BUILD_GRANT,
        scratch=[
            pltpu.VMEM((slots, TILE, TILE), BF),
            pltpu.SemaphoreType.DMA((CHUNKS,)),
        ],
    )
    other = lax.ppermute(own, C, swap)
    part, hop, kept = call(
        functools.partial(first_own_kernel, row_block),
        (f32(dests, ROOTS), hops, f32(PV, ROOTS)),
        [VMEM] * 2,
        root_ids[None],
        own,
    )
    sent = call(
        functools.partial(first_other_kernel, row_block),
        bf(dests, ROOTS),
        [VMEM] * 3,
        root_ids[None],
        other,
        part,
    )
    for level in range(1, LEVELS):
        parts = exchanged(sent.reshape(z_all, PV, ROOTS), Z)
        hop, kept, front = call(
            functools.partial(update_kernel, level),
            (hops, f32(PV, ROOTS), bf(rows_all, PV, ROOTS)),
            [VMEM] * 3,
            parts,
            hop,
            kept,
        )
        front = exchanged(front, ROW).reshape(sources, ROOTS)
        sent = call(level_kernel, bf(dests, ROOTS), [VMEM] * 3, front, own, other)
    parts = exchanged(sent.reshape(z_all, PV, ROOTS), Z)
    mine, theirs, sums = call(
        last_kernel,
        (f32(PV, ROOTS), f32(PV, ROOTS), f32(z_all, LEVELS, ROOTS)),
        [VMEM] * 3,
        parts,
        hop,
        kept,
    )
    theirs = lax.ppermute(theirs, C, swap)
    sums = exchanged(sums, Z)
    sums = call(sum_kernel, f32(2 * rows_all, LEVELS, ROOTS), [VMEM], sums)
    sums = exchanged(sums, (Y, X, C))
    return call(end_kernel, (hops, f32(PV, ROOTS), f32(LEVELS, ROOTS)), [VMEM] * 3, sums, mine, theirs)


def solution(mesh):
    torus = Mesh(mesh.devices.reshape(4, 4, 16, 2), (Y, X, Z, C))
    return jax.shard_map(
        local,
        mesh=torus,
        in_specs=(P(ROW, COL, None, None, None), P(ROW, COL, None, None), P(ROW, COL), P()),
        out_specs=(P((Y, X, Z, C), None), P((Y, X, Z, C), None), P()),
        check_vma=False,
    )
```

```python
import functools

import jax
import jax.numpy as jnp
from jax import lax
from jax.experimental import pallas as pl
from jax.experimental.pallas import tpu as pltpu
from jax.sharding import Mesh
from jax.sharding import PartitionSpec as P

ROOTS = 128
HALF = ROOTS // 2
PV = 32
LEVELS = 4
TILE = 128
GRANT = 8 << 20
CHUNKS = 4
Y, X, Z, C = "y", "x", "z", "c"
ROW = (Y, X)
COL = (Z, C)
VMEM = pl.BlockSpec(memory_space=pltpu.VMEM)
SMEM = pl.BlockSpec(memory_space=pltpu.SMEM)
ANY = pl.BlockSpec(memory_space=pl.ANY)
BF = jnp.bfloat16
F32 = jnp.float32


def call(kernel, out_shape, in_specs, *operands, scratch=()):
    return pl.pallas_call(
        kernel,
        out_shape=out_shape,
        in_specs=in_specs,
        out_specs=jax.tree.map(lambda _: VMEM, out_shape),
        scratch_shapes=scratch,
        compiler_params=pltpu.CompilerParams(vmem_limit_bytes=GRANT),
    )(*operands)


def build_kernel(total_ref, pos_hbm, tiles_hbm, dense_ref, pos_ref, tiles_ref, pos_sem, tile_sems):
    columns = dense_ref.shape[1] // 2
    core = lax.axis_index(C)
    slots = tiles_ref.shape[0]
    step = slots // CHUNKS
    pos_copy = pltpu.make_async_copy(pos_hbm, pos_ref, pos_sem)
    pos_copy.start()
    tile_copies = []
    for chunk in range(CHUNKS):
        part = pl.ds(chunk * step, step)
        tile_copies.append(pltpu.make_async_copy(tiles_hbm.at[part], tiles_ref.at[part], tile_sems.at[chunk]))
        tile_copies[-1].start()
    dense_ref[...] = jnp.zeros_like(dense_ref)

    def place(slot, carry):
        dest, source = pos_ref[0, slot], pos_ref[1, slot]
        for part in range(2):
            for half in range(2):
                first = pl.multiple_of(part * 2 * PV + (half ^ core) * PV, PV)
                rows = pl.multiple_of(dest * 2 * PV + part * PV, PV)
                lanes = pl.multiple_of(half * columns + source * TILE, TILE)
                dense_ref[pl.ds(rows, PV), pl.ds(lanes, TILE)] = tiles_ref[slot, pl.ds(first, PV), :]
        return carry

    pos_copy.wait()
    for chunk in range(CHUNKS):
        tile_copies[chunk].wait()
        lax.fori_loop(chunk * step, jnp.minimum(total_ref[0, 0], (chunk + 1) * step), place, 0)


def left_half(shape):
    return lax.broadcasted_iota(jnp.int32, shape, len(shape) - 1) < HALF


def own_roots(roots_ref):
    roots = roots_ref[...]
    turned = pltpu.roll(roots, HALF, 1)
    return jnp.where(left_half(roots.shape) == (lax.axis_index(C) == 0), roots, turned)


def times(ref, half, value):
    rows = value.shape[0]
    return jnp.dot(ref[:, half * rows : (half + 1) * rows], value.astype(BF), preferred_element_type=F32)


def own_products(own_ref, front, turned):
    left = left_half(front.shape)
    zero = jnp.zeros_like(front)
    return times(own_ref, 0, jnp.where(left, front, zero)) + times(own_ref, 1, jnp.where(left, zero, turned))


def other_products(other_ref, front, turned):
    left = left_half(front.shape)
    zero = jnp.zeros_like(front)
    return times(other_ref, 0, jnp.where(left, zero, front)) + times(other_ref, 1, jnp.where(left, turned, zero))


def root_front(row_block, roots_ref, sources):
    core, pair = lax.axis_index(C), lax.axis_index(Z) * 2 * PV
    base_own, base_other = pair + core * PV, pair + (1 - core) * PV
    roots = own_roots(roots_ref)
    shape = (sources, ROOTS)
    row = lax.broadcasted_iota(jnp.int32, shape, 0)
    left = left_half(shape)
    vertex = (row // PV) * row_block + row % PV
    front = (vertex + jnp.where(left, base_own, base_other) == roots).astype(F32)
    turned = (vertex + jnp.where(left, base_other, base_own) == roots).astype(F32)
    return front, turned


def first_own_kernel(row_block, roots_ref, own_ref, part_ref, hop_ref, kept_ref):
    front, turned = root_front(row_block, roots_ref, own_ref.shape[1] // 2)
    part_ref[...] = own_products(own_ref, front, turned)
    core, pair = lax.axis_index(C), lax.axis_index(Z) * 2 * PV
    base_own, base_other = pair + core * PV, pair + (1 - core) * PV
    state = hop_ref.shape
    vertex = lax.broadcasted_iota(jnp.int32, state, 0) + lax.axis_index(ROW) * row_block
    is_root = vertex + jnp.where(left_half(state), base_own, base_other) == own_roots(roots_ref)
    kept_ref[...] = is_root.astype(F32)
    hop_ref[...] = jnp.where(is_root, 0, LEVELS + 1)


def first_other_kernel(row_block, roots_ref, other_ref, part_ref, sent_ref):
    front, turned = root_front(row_block, roots_ref, other_ref.shape[1] // 2)
    sent_ref[...] = (part_ref[...] + other_products(other_ref, front, turned)).astype(BF)


def level_kernel(front_ref, own_ref, other_ref, sent_ref):
    front = front_ref[...].astype(F32)
    turned = pltpu.roll(front, HALF, 1)
    total = own_products(own_ref, front, turned) + other_products(other_ref, front, turned)
    sent_ref[...] = total.astype(BF)


def found(level, parts_ref, hop_ref, kept_ref):
    arrived = parts_ref[0].astype(F32)
    for peer in range(1, parts_ref.shape[0]):
        arrived += parts_ref[peer].astype(F32)
    hop = hop_ref[...]
    newly = (arrived > 0) & (hop == LEVELS + 1)
    path = jnp.where(newly, arrived, 0.0)
    return jnp.where(newly, level, hop), kept_ref[...] + path, path


def update_kernel(level, parts_ref, hop_in, kept_in, hop_ref, kept_ref, front_ref):
    hop_ref[...], kept_ref[...], path = found(level, parts_ref, hop_in, kept_in)
    path = path.astype(BF)
    for peer in range(front_ref.shape[0]):
        front_ref[peer] = path


def last_kernel(parts_ref, hop_in, kept_in, mine_ref, theirs_ref, sums_ref):
    hop, kept, _ = found(LEVELS, parts_ref, hop_in, kept_in)
    hops = hop.astype(F32)
    left = left_half(hop.shape)
    mine_ref[...] = jnp.where(left, hops, pltpu.roll(kept, HALF, 1))
    theirs_ref[...] = jnp.where(left, pltpu.roll(hops, HALF, 1), kept)
    sums = []
    for level in range(1, LEVELS + 1):
        at = hop == level
        count = jnp.sum(at.astype(F32), axis=0, keepdims=True)
        total = jnp.sum(jnp.where(at, kept, 0.0), axis=0, keepdims=True)
        count, total = count + pltpu.roll(count, HALF, 1), total + pltpu.roll(total, HALF, 1)
        sums.append(jnp.where(left_half(count.shape), count, total))
    sums = jnp.concatenate(sums, axis=0)
    for peer in range(sums_ref.shape[0]):
        sums_ref[peer] = sums


def sum_kernel(parts_ref, sums_ref):
    sums = jnp.sum(parts_ref[...], axis=0)
    for peer in range(sums_ref.shape[0]):
        sums_ref[peer] = sums


def end_kernel(sums_ref, mine_ref, theirs_ref, hop_ref, share_ref, counts_ref):
    parts = sums_ref[...]
    sums = jnp.sum(parts.reshape(parts.shape[0] // 2, 2, *parts.shape[1:]), axis=0)
    first, second = sums[0], sums[1]
    left = left_half(first.shape)
    counts = jnp.where(left, first, pltpu.roll(second, HALF, 1))
    totals = jnp.where(left, pltpu.roll(first, HALF, 1), second)
    counts_ref[...] = counts
    factor = counts / jnp.maximum(totals, 1.0)
    mine, theirs = mine_ref[...], theirs_ref[...]
    is_first = lax.axis_index(C) == 0
    low, high = jnp.where(is_first, mine, theirs), jnp.where(is_first, theirs, mine)
    left = left_half(low.shape)
    hop = jnp.where(left, low, pltpu.roll(high, HALF, 1)).astype(jnp.int32)
    kept = jnp.where(left, pltpu.roll(low, HALF, 1), high)
    scale = jnp.where(hop == 0, 1.0, 0.0)
    for level in range(1, LEVELS + 1):
        scale = jnp.where(hop == level, factor[level - 1 : level], scale)
    hop_ref[...] = hop
    share_ref[...] = kept * scale


def exchanged(value, axis):
    return lax.all_to_all(value, axis, 0, 0, tiled=True)


def local(tile_weights, tile_pos, tile_total, root_ids):
    rows_all, z_all = lax.axis_size(ROW), lax.axis_size(Z)
    row_block, sources, dests = z_all * 2 * PV, rows_all * PV, z_all * PV
    bf = lambda *shape: jax.ShapeDtypeStruct(shape, BF)
    f32 = lambda *shape: jax.ShapeDtypeStruct(shape, F32)
    hops = jax.ShapeDtypeStruct((PV, ROOTS), jnp.int32)
    swap = [(0, 1), (1, 0)]

    slots = tile_weights.shape[2]
    own = call(
        build_kernel,
        bf(dests, 2 * sources),
        [SMEM, ANY, ANY],
        tile_total,
        pltpu.with_memory_space_constraint(tile_pos[0, 0], pltpu.HBM),
        pltpu.with_memory_space_constraint(tile_weights[0, 0], pltpu.HBM),
        scratch=[
            pltpu.SMEM((2, slots), jnp.int32),
            pltpu.VMEM((slots, TILE, TILE), BF),
            pltpu.SemaphoreType.DMA,
            pltpu.SemaphoreType.DMA((CHUNKS,)),
        ],
    )
    other = lax.ppermute(own, C, swap)
    part, hop, kept = call(
        functools.partial(first_own_kernel, row_block),
        (f32(dests, ROOTS), hops, f32(PV, ROOTS)),
        [VMEM] * 2,
        root_ids[None],
        own,
    )
    sent = call(
        functools.partial(first_other_kernel, row_block),
        bf(dests, ROOTS),
        [VMEM] * 3,
        root_ids[None],
        other,
        part,
    )
    for level in range(1, LEVELS):
        parts = exchanged(sent.reshape(z_all, PV, ROOTS), Z)
        hop, kept, front = call(
            functools.partial(update_kernel, level),
            (hops, f32(PV, ROOTS), bf(rows_all, PV, ROOTS)),
            [VMEM] * 3,
            parts,
            hop,
            kept,
        )
        front = exchanged(front, ROW).reshape(sources, ROOTS)
        sent = call(level_kernel, bf(dests, ROOTS), [VMEM] * 3, front, own, other)
    parts = exchanged(sent.reshape(z_all, PV, ROOTS), Z)
    mine, theirs, sums = call(
        last_kernel,
        (f32(PV, ROOTS), f32(PV, ROOTS), f32(z_all, LEVELS, ROOTS)),
        [VMEM] * 3,
        parts,
        hop,
        kept,
    )
    theirs = lax.ppermute(theirs, C, swap)
    sums = exchanged(sums, Z)
    sums = call(sum_kernel, f32(2 * rows_all, LEVELS, ROOTS), [VMEM], sums)
    sums = exchanged(sums, (Y, X, C))
    return call(end_kernel, (hops, f32(PV, ROOTS), f32(LEVELS, ROOTS)), [VMEM] * 3, sums, mine, theirs)


def solution(mesh):
    torus = Mesh(mesh.devices.reshape(4, 4, 16, 2), (Y, X, Z, C))
    return jax.shard_map(
        local,
        mesh=torus,
        in_specs=(P(ROW, COL, None, None, None), P(ROW, COL, None, None), P(ROW, COL), P()),
        out_specs=(P((Y, X, Z, C), None), P((Y, X, Z, C), None), P()),
        check_vma=False,
    )
```

```python
import functools

import jax
import jax.numpy as jnp
from jax import lax
from jax.experimental import pallas as pl
from jax.experimental.pallas import tpu as pltpu
from jax.sharding import Mesh
from jax.sharding import PartitionSpec as P

ROOTS = 128
HALF = ROOTS // 2
PV = 32
LEVELS = 4
TILE = 128
GRANT = 8 << 20
CHUNKS = 4
Y, X, Z, C = "y", "x", "z", "c"
ROW = (Y, X)
COL = (Z, C)
VMEM = pl.BlockSpec(memory_space=pltpu.VMEM)
SMEM = pl.BlockSpec(memory_space=pltpu.SMEM)
ANY = pl.BlockSpec(memory_space=pl.ANY)
BF = jnp.bfloat16
F32 = jnp.float32


def call(kernel, out_shape, in_specs, *operands, scratch=()):
    return pl.pallas_call(
        kernel,
        out_shape=out_shape,
        in_specs=in_specs,
        out_specs=jax.tree.map(lambda _: VMEM, out_shape),
        scratch_shapes=scratch,
        compiler_params=pltpu.CompilerParams(vmem_limit_bytes=GRANT),
    )(*operands)


def start_kernel(
    row_block,
    total_ref,
    pos_hbm,
    tiles_hbm,
    roots_hbm,
    near_ref,
    far_ref,
    mine_ref,
    theirs_ref,
    hop_ref,
    kept_ref,
    pos_ref,
    tiles_ref,
    roots_ref,
    pos_sem,
    roots_sem,
    tile_sems,
):
    core = lax.axis_index(C)
    slots = tiles_ref.shape[0]
    step = slots // CHUNKS
    pos_copy = pltpu.make_async_copy(pos_hbm, pos_ref, pos_sem)
    pos_copy.start()
    roots_copy = pltpu.make_async_copy(roots_hbm, roots_ref, roots_sem)
    roots_copy.start()
    tile_copies = []
    for chunk in range(CHUNKS):
        part = pl.ds(chunk * step, step)
        tile_copies.append(pltpu.make_async_copy(tiles_hbm.at[part], tiles_ref.at[part], tile_sems.at[chunk]))
        tile_copies[-1].start()
    for block_ref in (near_ref, far_ref):
        block_ref[...] = jnp.zeros_like(block_ref)

    def place(slot, carry):
        dest, source = pos_ref[0, slot], pos_ref[1, slot]
        for part in range(2):
            for half, block_ref in enumerate((near_ref, far_ref)):
                first = pl.multiple_of(part * 2 * PV + (half ^ core) * PV, PV)
                rows = pl.multiple_of(dest * 2 * PV + part * PV, PV)
                lanes = pl.multiple_of(source * TILE, TILE)
                block_ref[pl.ds(rows, PV), pl.ds(lanes, TILE)] = tiles_ref[slot, pl.ds(first, PV), :]
        return carry

    pos_copy.wait()
    for chunk in range(CHUNKS):
        tile_copies[chunk].wait()
        lax.fori_loop(chunk * step, jnp.minimum(total_ref[0, 0], (chunk + 1) * step), place, 0)

    roots_copy.wait()
    first_products(row_block, roots_ref, near_ref, far_ref, mine_ref, theirs_ref, hop_ref, kept_ref)


def left_half(shape):
    return lax.broadcasted_iota(jnp.int32, shape, len(shape) - 1) < HALF


def own_roots(roots_ref):
    roots = roots_ref[...]
    return jnp.where(lax.axis_index(C) == 0, roots, pltpu.roll(roots, HALF, 1))


def times(ref, value):
    return jnp.dot(ref[...], value.astype(BF), preferred_element_type=F32)


def own_products(near_ref, far_ref, front, turned):
    left = left_half(front.shape)
    zero = jnp.zeros_like(front)
    return times(near_ref, jnp.where(left, front, zero)) + times(far_ref, jnp.where(left, zero, turned))


def other_products(near_ref, far_ref, front, turned):
    left = left_half(front.shape)
    zero = jnp.zeros_like(front)
    return times(near_ref, jnp.where(left, zero, front)) + times(far_ref, jnp.where(left, turned, zero))


def first_products(row_block, roots_ref, near_ref, far_ref, mine_ref, theirs_ref, hop_ref, kept_ref):
    core, pair = lax.axis_index(C), lax.axis_index(Z) * 2 * PV
    base_own, base_other = pair + core * PV, pair + (1 - core) * PV
    roots = own_roots(roots_ref)
    turned = pltpu.roll(roots, HALF, 1)
    shape = (near_ref.shape[1], ROOTS)
    row = lax.broadcasted_iota(jnp.int32, shape, 0)
    vertex = (row // PV) * row_block + row % PV + base_own
    near = times(near_ref, (vertex == roots).astype(F32))
    far = times(far_ref, (vertex == turned).astype(F32))
    left = left_half(near.shape)
    mine_ref[...] = jnp.where(left, near, far).astype(BF)
    theirs_ref[...] = jnp.where(left, far, near).astype(BF)
    state = hop_ref.shape
    left = left_half(state)
    vertex = lax.broadcasted_iota(jnp.int32, state, 0) + lax.axis_index(ROW) * row_block
    is_root = vertex + jnp.where(left, base_own, base_other) == jnp.where(left, roots, turned)
    kept_ref[...] = is_root.astype(F32)
    hop_ref[...] = jnp.where(is_root, 0, LEVELS + 1)


def add_kernel(mine_ref, both_ref, sent_ref):
    sent_ref[...] = (mine_ref[...].astype(F32) + both_ref[1 - lax.axis_index(C)].astype(F32)).astype(BF)


def level_kernel(front_ref, own_near, own_far, other_near, other_far, sent_ref):
    front = front_ref[...].astype(F32)
    turned = pltpu.roll(front, HALF, 1)
    total = own_products(own_near, own_far, front, turned)
    total += other_products(other_near, other_far, front, turned)
    sent_ref[...] = total.astype(BF)


def found(level, parts_ref, hop_ref, kept_ref):
    arrived = parts_ref[0].astype(F32)
    for peer in range(1, parts_ref.shape[0]):
        arrived += parts_ref[peer].astype(F32)
    hop = hop_ref[...]
    newly = (arrived > 0) & (hop == LEVELS + 1)
    path = jnp.where(newly, arrived, 0.0)
    return jnp.where(newly, level, hop), kept_ref[...] + path, path


def update_kernel(level, parts_ref, hop_in, kept_in, hop_ref, kept_ref, front_ref):
    hop_ref[...], kept_ref[...], path = found(level, parts_ref, hop_in, kept_in)
    path = path.astype(BF)
    for peer in range(front_ref.shape[0]):
        front_ref[peer] = path


def last_kernel(parts_ref, hop_in, kept_in, mine_ref, theirs_ref, sums_ref):
    hop, kept, _ = found(LEVELS, parts_ref, hop_in, kept_in)
    hops = hop.astype(F32)
    left = left_half(hop.shape)
    mine_ref[...] = jnp.where(left, hops, pltpu.roll(kept, HALF, 1))
    theirs_ref[...] = jnp.where(left, pltpu.roll(hops, HALF, 1), kept)
    sums = []
    for level in range(1, LEVELS + 1):
        at = hop == level
        count = jnp.sum(at.astype(F32), axis=0, keepdims=True)
        total = jnp.sum(jnp.where(at, kept, 0.0), axis=0, keepdims=True)
        count, total = count + pltpu.roll(count, HALF, 1), total + pltpu.roll(total, HALF, 1)
        sums.append(jnp.where(left_half(count.shape), count, total))
    sums = jnp.concatenate(sums, axis=0)
    for peer in range(sums_ref.shape[0]):
        sums_ref[peer] = sums


def sum_kernel(parts_ref, sums_ref):
    sums = jnp.sum(parts_ref[...], axis=0)
    for peer in range(sums_ref.shape[0]):
        sums_ref[peer] = sums


def end_kernel(sums_ref, mine_ref, theirs_ref, hop_ref, share_ref, counts_ref):
    parts = sums_ref[...]
    sums = jnp.sum(parts.reshape(parts.shape[0] // 2, 2, *parts.shape[1:]), axis=0)
    first, second = sums[0], sums[1]
    left = left_half(first.shape)
    counts = jnp.where(left, first, pltpu.roll(second, HALF, 1))
    totals = jnp.where(left, pltpu.roll(first, HALF, 1), second)
    counts_ref[...] = counts
    factor = counts / jnp.maximum(totals, 1.0)
    mine, theirs = mine_ref[...], theirs_ref[...]
    is_first = lax.axis_index(C) == 0
    low, high = jnp.where(is_first, mine, theirs), jnp.where(is_first, theirs, mine)
    left = left_half(low.shape)
    hop = jnp.where(left, low, pltpu.roll(high, HALF, 1)).astype(jnp.int32)
    kept = jnp.where(left, pltpu.roll(low, HALF, 1), high)
    scale = jnp.where(hop == 0, 1.0, 0.0)
    for level in range(1, LEVELS + 1):
        scale = jnp.where(hop == level, factor[level - 1 : level], scale)
    hop_ref[...] = hop
    share_ref[...] = kept * scale


def exchanged(value, axis):
    return lax.all_to_all(value, axis, 0, 0, tiled=True)


def local(tile_weights, tile_pos, tile_total, root_ids):
    rows_all, z_all = lax.axis_size(ROW), lax.axis_size(Z)
    row_block, sources, dests = z_all * 2 * PV, rows_all * PV, z_all * PV
    bf = lambda *shape: jax.ShapeDtypeStruct(shape, BF)
    f32 = lambda *shape: jax.ShapeDtypeStruct(shape, F32)
    hops = jax.ShapeDtypeStruct((PV, ROOTS), jnp.int32)
    swap = [(0, 1), (1, 0)]

    slots = tile_weights.shape[2]
    held = lambda value: pltpu.with_memory_space_constraint(value, pltpu.HBM)
    near, far, mine, theirs, hop, kept = call(
        functools.partial(start_kernel, row_block),
        (bf(dests, sources), bf(dests, sources), bf(dests, ROOTS), bf(dests, ROOTS), hops, f32(PV, ROOTS)),
        [SMEM, ANY, ANY, ANY],
        tile_total,
        held(tile_pos[0, 0]),
        held(tile_weights[0, 0]),
        held(root_ids[None]),
        scratch=[
            pltpu.SMEM((2, slots), jnp.int32),
            pltpu.VMEM((slots, TILE, TILE), BF),
            pltpu.VMEM((1, ROOTS), jnp.int32),
            pltpu.SemaphoreType.DMA,
            pltpu.SemaphoreType.DMA,
            pltpu.SemaphoreType.DMA((CHUNKS,)),
        ],
    )
    both = lax.all_gather(theirs, C)
    blocks = (near, far, lax.ppermute(near, C, swap), lax.ppermute(far, C, swap))
    sent = call(add_kernel, bf(dests, ROOTS), [VMEM] * 2, mine, both)
    for level in range(1, LEVELS):
        parts = exchanged(sent.reshape(z_all, PV, ROOTS), Z)
        hop, kept, front = call(
            functools.partial(update_kernel, level),
            (hops, f32(PV, ROOTS), bf(rows_all, PV, ROOTS)),
            [VMEM] * 3,
            parts,
            hop,
            kept,
        )
        front = exchanged(front, ROW).reshape(sources, ROOTS)
        sent = call(level_kernel, bf(dests, ROOTS), [VMEM] * 5, front, *blocks)
    parts = exchanged(sent.reshape(z_all, PV, ROOTS), Z)
    mine, theirs, sums = call(
        last_kernel,
        (f32(PV, ROOTS), f32(PV, ROOTS), f32(z_all, LEVELS, ROOTS)),
        [VMEM] * 3,
        parts,
        hop,
        kept,
    )
    theirs = lax.ppermute(theirs, C, swap)
    sums = exchanged(sums, Z)
    sums = call(sum_kernel, f32(2 * rows_all, LEVELS, ROOTS), [VMEM], sums)
    sums = exchanged(sums, (Y, X, C))
    return call(end_kernel, (hops, f32(PV, ROOTS), f32(LEVELS, ROOTS)), [VMEM] * 3, sums, mine, theirs)


def solution(mesh):
    torus = Mesh(mesh.devices.reshape(4, 4, 16, 2), (Y, X, Z, C))
    return jax.shard_map(
        local,
        mesh=torus,
        in_specs=(P(ROW, COL, None, None, None), P(ROW, COL, None, None), P(ROW, COL), P()),
        out_specs=(P((Y, X, Z, C), None), P((Y, X, Z, C), None), P()),
        check_vma=False,
    )
```

```python
import functools

import jax
import jax.numpy as jnp
from jax import lax
from jax.experimental import pallas as pl
from jax.experimental.pallas import tpu as pltpu
from jax.sharding import Mesh
from jax.sharding import PartitionSpec as P

ROOTS = 128
HALF = ROOTS // 2
PV = 32
LEVELS = 4
TILE = 128
GRANT = 8 << 20
CHUNKS = 4
Y, X, Z, C = "y", "x", "z", "c"
ROW = (Y, X)
COL = (Z, C)
VMEM = pl.BlockSpec(memory_space=pltpu.VMEM)
SMEM = pl.BlockSpec(memory_space=pltpu.SMEM)
ANY = pl.BlockSpec(memory_space=pl.ANY)
BF = jnp.bfloat16
F32 = jnp.float32


def call(kernel, out_shape, in_specs, *operands, scratch=()):
    return pl.pallas_call(
        kernel,
        out_shape=out_shape,
        in_specs=in_specs,
        out_specs=jax.tree.map(lambda _: VMEM, out_shape),
        scratch_shapes=scratch,
        compiler_params=pltpu.CompilerParams(vmem_limit_bytes=GRANT),
    )(*operands)


def start_kernel(
    row_block,
    total_ref,
    pos_hbm,
    tiles_hbm,
    roots_hbm,
    near_ref,
    far_ref,
    mine_ref,
    theirs_ref,
    hop_ref,
    kept_ref,
    pos_ref,
    tiles_ref,
    roots_ref,
    pos_sem,
    roots_sem,
    tile_sems,
):
    core = lax.axis_index(C)
    slots = tiles_ref.shape[0]
    step = slots // CHUNKS
    pos_copy = pltpu.make_async_copy(pos_hbm, pos_ref, pos_sem)
    pos_copy.start()
    roots_copy = pltpu.make_async_copy(roots_hbm, roots_ref, roots_sem)
    roots_copy.start()
    tile_copies = []
    for chunk in range(CHUNKS):
        part = pl.ds(chunk * step, step)
        tile_copies.append(pltpu.make_async_copy(tiles_hbm.at[part], tiles_ref.at[part], tile_sems.at[chunk]))
        tile_copies[-1].start()
    for block_ref in (near_ref, far_ref):
        block_ref[...] = jnp.zeros_like(block_ref)

    def place(slot, carry):
        dest, source = pos_ref[0, slot], pos_ref[1, slot]
        for part in range(2):
            for half, block_ref in enumerate((near_ref, far_ref)):
                first = pl.multiple_of(part * 2 * PV + (half ^ core) * PV, PV)
                rows = pl.multiple_of(dest * 2 * PV + part * PV, PV)
                lanes = pl.multiple_of(source * TILE, TILE)
                block_ref[pl.ds(rows, PV), pl.ds(lanes, TILE)] = tiles_ref[slot, pl.ds(first, PV), :]
        return carry

    pos_copy.wait()
    for chunk in range(CHUNKS):
        tile_copies[chunk].wait()
        lax.fori_loop(chunk * step, jnp.minimum(total_ref[0, 0], (chunk + 1) * step), place, 0)

    roots_copy.wait()
    first_products(row_block, roots_ref, near_ref, far_ref, mine_ref, theirs_ref, hop_ref, kept_ref)


def left_half(shape):
    return lax.broadcasted_iota(jnp.int32, shape, len(shape) - 1) < HALF


def own_roots(roots_ref):
    roots = roots_ref[...]
    return jnp.where(lax.axis_index(C) == 0, roots, pltpu.roll(roots, HALF, 1))


def times(ref, value):
    return jnp.dot(ref[...], value.astype(BF), preferred_element_type=F32)


def own_products(near_ref, far_ref, front, turned):
    left = left_half(front.shape)
    zero = jnp.zeros_like(front)
    return times(near_ref, jnp.where(left, front, zero)) + times(far_ref, jnp.where(left, zero, turned))


def other_products(near_ref, far_ref, front, turned):
    left = left_half(front.shape)
    zero = jnp.zeros_like(front)
    return times(near_ref, jnp.where(left, zero, front)) + times(far_ref, jnp.where(left, turned, zero))


def first_products(row_block, roots_ref, near_ref, far_ref, mine_ref, theirs_ref, hop_ref, kept_ref):
    core, pair = lax.axis_index(C), lax.axis_index(Z) * 2 * PV
    base_own, base_other = pair + core * PV, pair + (1 - core) * PV
    roots = own_roots(roots_ref)
    turned = pltpu.roll(roots, HALF, 1)
    shape = (near_ref.shape[1], ROOTS)
    row = lax.broadcasted_iota(jnp.int32, shape, 0)
    vertex = (row // PV) * row_block + row % PV + base_own
    near = times(near_ref, (vertex == roots).astype(F32))
    far = times(far_ref, (vertex == turned).astype(F32))
    left = left_half(near.shape)
    mine_ref[...] = jnp.where(left, near, far).astype(BF)
    theirs_ref[...] = jnp.where(left, far, near).astype(BF)
    state = hop_ref.shape
    left = left_half(state)
    vertex = lax.broadcasted_iota(jnp.int32, state, 0) + lax.axis_index(ROW) * row_block
    is_root = vertex + jnp.where(left, base_own, base_other) == jnp.where(left, roots, turned)
    kept_ref[...] = is_root.astype(F32)
    hop_ref[...] = jnp.where(is_root, 0, LEVELS + 1)


def add_kernel(mine_ref, both_ref, sent_ref):
    sent_ref[...] = (mine_ref[...].astype(F32) + both_ref[1 - lax.axis_index(C)].astype(F32)).astype(BF)


def level_kernel(front_ref, own_near, own_far, other_near, other_far, sent_ref):
    front = front_ref[...].astype(F32)
    turned = pltpu.roll(front, HALF, 1)
    total = own_products(own_near, own_far, front, turned)
    total += other_products(other_near, other_far, front, turned)
    sent_ref[...] = total.astype(BF)


def own_kernel(front_ref, own_near, own_far, part_ref):
    front = front_ref[...].astype(F32)
    part_ref[...] = own_products(own_near, own_far, front, pltpu.roll(front, HALF, 1))


def other_kernel(front_ref, part_ref, other_near, other_far, sent_ref):
    front = front_ref[...].astype(F32)
    total = part_ref[...] + other_products(other_near, other_far, front, pltpu.roll(front, HALF, 1))
    sent_ref[...] = total.astype(BF)


def found(level, parts_ref, hop_ref, kept_ref):
    arrived = parts_ref[0].astype(F32)
    for peer in range(1, parts_ref.shape[0]):
        arrived += parts_ref[peer].astype(F32)
    hop = hop_ref[...]
    newly = (arrived > 0) & (hop == LEVELS + 1)
    path = jnp.where(newly, arrived, 0.0)
    return jnp.where(newly, level, hop), kept_ref[...] + path, path


def update_kernel(level, parts_ref, hop_in, kept_in, hop_ref, kept_ref, front_ref):
    hop_ref[...], kept_ref[...], path = found(level, parts_ref, hop_in, kept_in)
    path = path.astype(BF)
    for peer in range(front_ref.shape[0]):
        front_ref[peer] = path


def last_kernel(parts_ref, hop_in, kept_in, mine_ref, theirs_ref, sums_ref):
    hop, kept, _ = found(LEVELS, parts_ref, hop_in, kept_in)
    hops = hop.astype(F32)
    left = left_half(hop.shape)
    mine_ref[...] = jnp.where(left, hops, pltpu.roll(kept, HALF, 1))
    theirs_ref[...] = jnp.where(left, pltpu.roll(hops, HALF, 1), kept)
    sums = []
    for level in range(1, LEVELS + 1):
        at = hop == level
        count = jnp.sum(at.astype(F32), axis=0, keepdims=True)
        total = jnp.sum(jnp.where(at, kept, 0.0), axis=0, keepdims=True)
        count, total = count + pltpu.roll(count, HALF, 1), total + pltpu.roll(total, HALF, 1)
        sums.append(jnp.where(left_half(count.shape), count, total))
    sums = jnp.concatenate(sums, axis=0)
    for peer in range(sums_ref.shape[0]):
        sums_ref[peer] = sums


def sum_kernel(parts_ref, sums_ref):
    sums = jnp.sum(parts_ref[...], axis=0)
    for peer in range(sums_ref.shape[0]):
        sums_ref[peer] = sums


def end_kernel(sums_ref, mine_ref, theirs_ref, hop_ref, share_ref, counts_ref):
    parts = sums_ref[...]
    sums = jnp.sum(parts.reshape(parts.shape[0] // 2, 2, *parts.shape[1:]), axis=0)
    first, second = sums[0], sums[1]
    left = left_half(first.shape)
    counts = jnp.where(left, first, pltpu.roll(second, HALF, 1))
    totals = jnp.where(left, pltpu.roll(first, HALF, 1), second)
    counts_ref[...] = counts
    factor = counts / jnp.maximum(totals, 1.0)
    mine, theirs = mine_ref[...], theirs_ref[...]
    is_first = lax.axis_index(C) == 0
    low, high = jnp.where(is_first, mine, theirs), jnp.where(is_first, theirs, mine)
    left = left_half(low.shape)
    hop = jnp.where(left, low, pltpu.roll(high, HALF, 1)).astype(jnp.int32)
    kept = jnp.where(left, pltpu.roll(low, HALF, 1), high)
    scale = jnp.where(hop == 0, 1.0, 0.0)
    for level in range(1, LEVELS + 1):
        scale = jnp.where(hop == level, factor[level - 1 : level], scale)
    hop_ref[...] = hop
    share_ref[...] = kept * scale


def exchanged(value, axis):
    return lax.all_to_all(value, axis, 0, 0, tiled=True)


def local(tile_weights, tile_pos, tile_total, root_ids):
    rows_all, z_all = lax.axis_size(ROW), lax.axis_size(Z)
    row_block, sources, dests = z_all * 2 * PV, rows_all * PV, z_all * PV
    bf = lambda *shape: jax.ShapeDtypeStruct(shape, BF)
    f32 = lambda *shape: jax.ShapeDtypeStruct(shape, F32)
    hops = jax.ShapeDtypeStruct((PV, ROOTS), jnp.int32)
    swap = [(0, 1), (1, 0)]

    slots = tile_weights.shape[2]
    held = lambda value: pltpu.with_memory_space_constraint(value, pltpu.HBM)
    near, far, mine, theirs, hop, kept = call(
        functools.partial(start_kernel, row_block),
        (bf(dests, sources), bf(dests, sources), bf(dests, ROOTS), bf(dests, ROOTS), hops, f32(PV, ROOTS)),
        [SMEM, ANY, ANY, ANY],
        tile_total,
        held(tile_pos[0, 0]),
        held(tile_weights[0, 0]),
        held(root_ids[None]),
        scratch=[
            pltpu.SMEM((2, slots), jnp.int32),
            pltpu.VMEM((slots, TILE, TILE), BF),
            pltpu.VMEM((1, ROOTS), jnp.int32),
            pltpu.SemaphoreType.DMA,
            pltpu.SemaphoreType.DMA,
            pltpu.SemaphoreType.DMA((CHUNKS,)),
        ],
    )
    both = lax.all_gather(theirs, C)
    blocks = (near, far, lax.ppermute(near, C, swap), lax.ppermute(far, C, swap))
    sent = call(add_kernel, bf(dests, ROOTS), [VMEM] * 2, mine, both)
    for level in range(1, LEVELS):
        parts = exchanged(sent.reshape(z_all, PV, ROOTS), Z)
        hop, kept, front = call(
            functools.partial(update_kernel, level),
            (hops, f32(PV, ROOTS), bf(rows_all, PV, ROOTS)),
            [VMEM] * 3,
            parts,
            hop,
            kept,
        )
        front = exchanged(front, ROW).reshape(sources, ROOTS)
        if level == 1:
            part = call(own_kernel, f32(dests, ROOTS), [VMEM] * 3, front, *blocks[:2])
            sent = call(other_kernel, bf(dests, ROOTS), [VMEM] * 4, front, part, *blocks[2:])
        else:
            sent = call(level_kernel, bf(dests, ROOTS), [VMEM] * 5, front, *blocks)
    parts = exchanged(sent.reshape(z_all, PV, ROOTS), Z)
    mine, theirs, sums = call(
        last_kernel,
        (f32(PV, ROOTS), f32(PV, ROOTS), f32(z_all, LEVELS, ROOTS)),
        [VMEM] * 3,
        parts,
        hop,
        kept,
    )
    theirs = lax.ppermute(theirs, C, swap)
    sums = exchanged(sums, Z)
    sums = call(sum_kernel, f32(2 * rows_all, LEVELS, ROOTS), [VMEM], sums)
    sums = exchanged(sums, (Y, X, C))
    return call(end_kernel, (hops, f32(PV, ROOTS), f32(LEVELS, ROOTS)), [VMEM] * 3, sums, mine, theirs)


def solution(mesh):
    torus = Mesh(mesh.devices.reshape(4, 4, 16, 2), (Y, X, Z, C))
    return jax.shard_map(
        local,
        mesh=torus,
        in_specs=(P(ROW, COL, None, None, None), P(ROW, COL, None, None), P(ROW, COL), P()),
        out_specs=(P((Y, X, Z, C), None), P((Y, X, Z, C), None), P()),
        check_vma=False,
    )
```

```python
import functools

import jax
import jax.numpy as jnp
from jax import lax
from jax.experimental import pallas as pl
from jax.experimental.pallas import tpu as pltpu
from jax.sharding import Mesh
from jax.sharding import PartitionSpec as P

ROOTS = 128
HALF = ROOTS // 2
PV = 32
LEVELS = 4
TILE = 128
GRANT = 8 << 20
CHUNKS = 4
Y, X, Z, C = "y", "x", "z", "c"
ROW = (Y, X)
COL = (Z, C)
VMEM = pl.BlockSpec(memory_space=pltpu.VMEM)
SMEM = pl.BlockSpec(memory_space=pltpu.SMEM)
ANY = pl.BlockSpec(memory_space=pl.ANY)
BF = jnp.bfloat16
F32 = jnp.float32


def call(kernel, out_shape, in_specs, *operands, scratch=()):
    return pl.pallas_call(
        kernel,
        out_shape=out_shape,
        in_specs=in_specs,
        out_specs=jax.tree.map(lambda _: VMEM, out_shape),
        scratch_shapes=scratch,
        compiler_params=pltpu.CompilerParams(vmem_limit_bytes=GRANT),
    )(*operands)


def start_kernel(
    row_block,
    total_ref,
    pos_hbm,
    tiles_hbm,
    roots_hbm,
    near_ref,
    far_ref,
    mine_ref,
    theirs_ref,
    hop_ref,
    kept_ref,
    pos_ref,
    tiles_ref,
    roots_ref,
    values_ref,
    pos_sem,
    roots_sem,
    tile_sems,
):
    core = lax.axis_index(C)
    slots = tiles_ref.shape[0]
    step = slots // CHUNKS
    pos_copy = pltpu.make_async_copy(pos_hbm, pos_ref, pos_sem)
    pos_copy.start()
    roots_copy = pltpu.make_async_copy(roots_hbm, roots_ref, roots_sem)
    roots_copy.start()
    tile_copies = []
    for chunk in range(CHUNKS):
        part = pl.ds(chunk * step, step)
        tile_copies.append(pltpu.make_async_copy(tiles_hbm.at[part], tiles_ref.at[part], tile_sems.at[chunk]))
        tile_copies[-1].start()
    for block_ref in (near_ref, far_ref):
        block_ref[...] = jnp.zeros_like(block_ref)

    def place(slot, carry):
        dest, source = pos_ref[0, slot], pos_ref[1, slot]
        for part in range(2):
            for half, block_ref in enumerate((near_ref, far_ref)):
                first = pl.multiple_of(part * 2 * PV + (half ^ core) * PV, PV)
                rows = pl.multiple_of(dest * 2 * PV + part * PV, PV)
                lanes = pl.multiple_of(source * TILE, TILE)
                block_ref[pl.ds(rows, PV), pl.ds(lanes, TILE)] = tiles_ref[slot, pl.ds(first, PV), :]
        return carry

    roots_copy.wait()
    first_values(row_block, roots_ref, values_ref, hop_ref, kept_ref)
    pos_copy.wait()
    for chunk in range(CHUNKS):
        tile_copies[chunk].wait()
        lax.fori_loop(chunk * step, jnp.minimum(total_ref[0, 0], (chunk + 1) * step), place, 0)

    first_products(values_ref, near_ref, far_ref, mine_ref, theirs_ref)


def left_half(shape):
    return lax.broadcasted_iota(jnp.int32, shape, len(shape) - 1) < HALF


def own_roots(roots_ref):
    roots = roots_ref[...]
    return jnp.where(lax.axis_index(C) == 0, roots, pltpu.roll(roots, HALF, 1))


def times(ref, value):
    return jnp.dot(ref[...], value.astype(BF), preferred_element_type=F32)


def own_products(near_ref, far_ref, front, turned):
    left = left_half(front.shape)
    zero = jnp.zeros_like(front)
    return times(near_ref, jnp.where(left, front, zero)) + times(far_ref, jnp.where(left, zero, turned))


def other_products(near_ref, far_ref, front, turned):
    left = left_half(front.shape)
    zero = jnp.zeros_like(front)
    return times(near_ref, jnp.where(left, zero, front)) + times(far_ref, jnp.where(left, turned, zero))


def first_values(row_block, roots_ref, values_ref, hop_ref, kept_ref):
    core, pair = lax.axis_index(C), lax.axis_index(Z) * 2 * PV
    base_own, base_other = pair + core * PV, pair + (1 - core) * PV
    roots = own_roots(roots_ref)
    turned = pltpu.roll(roots, HALF, 1)
    row = lax.broadcasted_iota(jnp.int32, values_ref.shape[1:], 0)
    vertex = (row // PV) * row_block + row % PV + base_own
    values_ref[0] = (vertex == roots).astype(F32).astype(BF)
    values_ref[1] = (vertex == turned).astype(F32).astype(BF)
    state = hop_ref.shape
    left = left_half(state)
    vertex = lax.broadcasted_iota(jnp.int32, state, 0) + lax.axis_index(ROW) * row_block
    is_root = vertex + jnp.where(left, base_own, base_other) == jnp.where(left, roots, turned)
    kept_ref[...] = is_root.astype(F32)
    hop_ref[...] = jnp.where(is_root, 0, LEVELS + 1)


def first_products(values_ref, near_ref, far_ref, mine_ref, theirs_ref):
    near, far = times(near_ref, values_ref[0]), times(far_ref, values_ref[1])
    left = left_half(near.shape)
    mine_ref[...] = jnp.where(left, near, far).astype(BF)
    theirs_ref[...] = jnp.where(left, far, near).astype(BF)


def add_kernel(mine_ref, both_ref, sent_ref):
    sent_ref[...] = (mine_ref[...].astype(F32) + both_ref[1 - lax.axis_index(C)].astype(F32)).astype(BF)


def level_kernel(front_ref, own_near, own_far, other_near, other_far, sent_ref):
    front = front_ref[...].astype(F32)
    turned = pltpu.roll(front, HALF, 1)
    total = own_products(own_near, own_far, front, turned)
    total += other_products(other_near, other_far, front, turned)
    sent_ref[...] = total.astype(BF)


def own_kernel(front_ref, own_near, own_far, part_ref):
    front = front_ref[...].astype(F32)
    part_ref[...] = own_products(own_near, own_far, front, pltpu.roll(front, HALF, 1))


def other_kernel(front_ref, part_ref, other_near, other_far, sent_ref):
    front = front_ref[...].astype(F32)
    total = part_ref[...] + other_products(other_near, other_far, front, pltpu.roll(front, HALF, 1))
    sent_ref[...] = total.astype(BF)


def found(level, parts_ref, hop_ref, kept_ref):
    arrived = parts_ref[0].astype(F32)
    for peer in range(1, parts_ref.shape[0]):
        arrived += parts_ref[peer].astype(F32)
    hop = hop_ref[...]
    newly = (arrived > 0) & (hop == LEVELS + 1)
    path = jnp.where(newly, arrived, 0.0)
    return jnp.where(newly, level, hop), kept_ref[...] + path, path


def update_kernel(level, parts_ref, hop_in, kept_in, hop_ref, kept_ref, front_ref):
    hop_ref[...], kept_ref[...], path = found(level, parts_ref, hop_in, kept_in)
    path = path.astype(BF)
    for peer in range(front_ref.shape[0]):
        front_ref[peer] = path


def last_kernel(parts_ref, hop_in, kept_in, mine_ref, theirs_ref, sums_ref):
    hop, kept, _ = found(LEVELS, parts_ref, hop_in, kept_in)
    hops = hop.astype(F32)
    left = left_half(hop.shape)
    mine_ref[...] = jnp.where(left, hops, pltpu.roll(kept, HALF, 1))
    theirs_ref[...] = jnp.where(left, pltpu.roll(hops, HALF, 1), kept)
    sums = []
    for level in range(1, LEVELS + 1):
        at = hop == level
        count = jnp.sum(at.astype(F32), axis=0, keepdims=True)
        total = jnp.sum(jnp.where(at, kept, 0.0), axis=0, keepdims=True)
        count, total = count + pltpu.roll(count, HALF, 1), total + pltpu.roll(total, HALF, 1)
        sums.append(jnp.where(left_half(count.shape), count, total))
    sums = jnp.concatenate(sums, axis=0)
    for peer in range(sums_ref.shape[0]):
        sums_ref[peer] = sums


def sum_kernel(parts_ref, sums_ref):
    sums = jnp.sum(parts_ref[...], axis=0)
    for peer in range(sums_ref.shape[0]):
        sums_ref[peer] = sums


def end_kernel(sums_ref, mine_ref, theirs_ref, hop_ref, share_ref, counts_ref):
    parts = sums_ref[...]
    sums = jnp.sum(parts.reshape(parts.shape[0] // 2, 2, *parts.shape[1:]), axis=0)
    first, second = sums[0], sums[1]
    left = left_half(first.shape)
    counts = jnp.where(left, first, pltpu.roll(second, HALF, 1))
    totals = jnp.where(left, pltpu.roll(first, HALF, 1), second)
    counts_ref[...] = counts
    factor = counts / jnp.maximum(totals, 1.0)
    mine, theirs = mine_ref[...], theirs_ref[...]
    is_first = lax.axis_index(C) == 0
    low, high = jnp.where(is_first, mine, theirs), jnp.where(is_first, theirs, mine)
    left = left_half(low.shape)
    hop = jnp.where(left, low, pltpu.roll(high, HALF, 1)).astype(jnp.int32)
    kept = jnp.where(left, pltpu.roll(low, HALF, 1), high)
    scale = jnp.where(hop == 0, 1.0, 0.0)
    for level in range(1, LEVELS + 1):
        scale = jnp.where(hop == level, factor[level - 1 : level], scale)
    hop_ref[...] = hop
    share_ref[...] = kept * scale


def exchanged(value, axis):
    return lax.all_to_all(value, axis, 0, 0, tiled=True)


def local(tile_weights, tile_pos, tile_total, root_ids):
    rows_all, z_all = lax.axis_size(ROW), lax.axis_size(Z)
    row_block, sources, dests = z_all * 2 * PV, rows_all * PV, z_all * PV
    bf = lambda *shape: jax.ShapeDtypeStruct(shape, BF)
    f32 = lambda *shape: jax.ShapeDtypeStruct(shape, F32)
    hops = jax.ShapeDtypeStruct((PV, ROOTS), jnp.int32)
    swap = [(0, 1), (1, 0)]

    slots = tile_weights.shape[2]
    held = lambda value: pltpu.with_memory_space_constraint(value, pltpu.HBM)
    near, far, mine, theirs, hop, kept = call(
        functools.partial(start_kernel, row_block),
        (bf(dests, sources), bf(dests, sources), bf(dests, ROOTS), bf(dests, ROOTS), hops, f32(PV, ROOTS)),
        [SMEM, ANY, ANY, ANY],
        tile_total,
        held(tile_pos[0, 0]),
        held(tile_weights[0, 0]),
        held(root_ids[None]),
        scratch=[
            pltpu.SMEM((2, slots), jnp.int32),
            pltpu.VMEM((slots, TILE, TILE), BF),
            pltpu.VMEM((1, ROOTS), jnp.int32),
            pltpu.VMEM((2, sources, ROOTS), BF),
            pltpu.SemaphoreType.DMA,
            pltpu.SemaphoreType.DMA,
            pltpu.SemaphoreType.DMA((CHUNKS,)),
        ],
    )
    both = lax.all_gather(theirs, C)
    blocks = (near, far, lax.ppermute(near, C, swap), lax.ppermute(far, C, swap))
    sent = call(add_kernel, bf(dests, ROOTS), [VMEM] * 2, mine, both)
    for level in range(1, LEVELS):
        parts = exchanged(sent.reshape(z_all, PV, ROOTS), Z)
        hop, kept, front = call(
            functools.partial(update_kernel, level),
            (hops, f32(PV, ROOTS), bf(rows_all, PV, ROOTS)),
            [VMEM] * 3,
            parts,
            hop,
            kept,
        )
        front = exchanged(front, ROW).reshape(sources, ROOTS)
        if level == 1:
            part = call(own_kernel, f32(dests, ROOTS), [VMEM] * 3, front, *blocks[:2])
            sent = call(other_kernel, bf(dests, ROOTS), [VMEM] * 4, front, part, *blocks[2:])
        else:
            sent = call(level_kernel, bf(dests, ROOTS), [VMEM] * 5, front, *blocks)
    parts = exchanged(sent.reshape(z_all, PV, ROOTS), Z)
    mine, theirs, sums = call(
        last_kernel,
        (f32(PV, ROOTS), f32(PV, ROOTS), f32(z_all, LEVELS, ROOTS)),
        [VMEM] * 3,
        parts,
        hop,
        kept,
    )
    theirs = lax.ppermute(theirs, C, swap)
    sums, theirs = lax.optimization_barrier((exchanged(sums, Z), theirs))
    sums = call(sum_kernel, f32(2 * rows_all, LEVELS, ROOTS), [VMEM], sums)
    sums = exchanged(sums, (Y, X, C))
    return call(end_kernel, (hops, f32(PV, ROOTS), f32(LEVELS, ROOTS)), [VMEM] * 3, sums, mine, theirs)


def solution(mesh):
    torus = Mesh(mesh.devices.reshape(4, 4, 16, 2), (Y, X, Z, C))
    return jax.shard_map(
        local,
        mesh=torus,
        in_specs=(P(ROW, COL, None, None, None), P(ROW, COL, None, None), P(ROW, COL), P()),
        out_specs=(P((Y, X, Z, C), None), P((Y, X, Z, C), None), P()),
        check_vma=False,
    )
```

```python
import functools

import jax
import jax.numpy as jnp
from jax import lax
from jax.experimental import pallas as pl
from jax.experimental.pallas import tpu as pltpu
from jax.sharding import Mesh
from jax.sharding import PartitionSpec as P

ROOTS = 128
HALF = ROOTS // 2
PV = 32
LEVELS = 4
TILE = 128
GRANT = 8 << 20
CHUNKS = 4
Y, X, Z, C = "y", "x", "z", "c"
ROW = (Y, X)
COL = (Z, C)
VMEM = pl.BlockSpec(memory_space=pltpu.VMEM)
SMEM = pl.BlockSpec(memory_space=pltpu.SMEM)
ANY = pl.BlockSpec(memory_space=pl.ANY)
BF = jnp.bfloat16
F32 = jnp.float32


def call(kernel, out_shape, in_specs, *operands, scratch=()):
    return pl.pallas_call(
        kernel,
        out_shape=out_shape,
        in_specs=in_specs,
        out_specs=jax.tree.map(lambda _: VMEM, out_shape),
        scratch_shapes=scratch,
        compiler_params=pltpu.CompilerParams(vmem_limit_bytes=GRANT),
    )(*operands)


def start_kernel(
    row_block,
    total_ref,
    pos_hbm,
    tiles_hbm,
    roots_hbm,
    near_ref,
    far_ref,
    mine_ref,
    theirs_ref,
    hop_ref,
    kept_ref,
    pos_ref,
    tiles_ref,
    roots_ref,
    values_ref,
    pos_sem,
    roots_sem,
    tile_sems,
):
    core = lax.axis_index(C)
    slots = tiles_ref.shape[0]
    step = slots // CHUNKS
    pos_copy = pltpu.make_async_copy(pos_hbm, pos_ref, pos_sem)
    pos_copy.start()
    roots_copy = pltpu.make_async_copy(roots_hbm, roots_ref, roots_sem)
    roots_copy.start()
    tile_copies = []
    for chunk in range(CHUNKS):
        part = pl.ds(chunk * step, step)
        tile_copies.append(pltpu.make_async_copy(tiles_hbm.at[part], tiles_ref.at[part], tile_sems.at[chunk]))
    for copy in reversed(tile_copies):
        copy.start()
    for block_ref in (near_ref, far_ref):
        block_ref[...] = jnp.zeros_like(block_ref)

    roots_copy.wait()
    first_values(row_block, roots_ref, values_ref, hop_ref, kept_ref)
    pos_copy.wait()
    total = total_ref[0, 0]
    row_tiles, column_tiles = near_ref.shape[0] // (2 * PV), near_ref.shape[1] // TILE
    for chunk in reversed(range(CHUNKS)):
        tile_copies[chunk].wait()
        for slot in reversed(range(chunk * step, (chunk + 1) * step)):
            dest = jnp.minimum(pos_ref[0, slot], row_tiles - 1)
            source = jnp.minimum(pos_ref[1, slot], column_tiles - 1)
            lanes = pl.ds(pl.multiple_of(source * TILE, TILE), TILE)
            used = slot < total
            for part in range(2):
                for half, block_ref in enumerate((near_ref, far_ref)):
                    first = pl.multiple_of(part * 2 * PV + (half ^ core) * PV, PV)
                    rows = pl.multiple_of(dest * 2 * PV + part * PV, PV)
                    tile = tiles_ref[slot, pl.ds(first, PV), :]
                    block_ref[pl.ds(rows, PV), lanes] = jnp.where(used, tile, jnp.zeros_like(tile))

    first_products(values_ref, near_ref, far_ref, mine_ref, theirs_ref)


def left_half(shape):
    return lax.broadcasted_iota(jnp.int32, shape, len(shape) - 1) < HALF


def own_roots(roots_ref):
    roots = roots_ref[...]
    return jnp.where(lax.axis_index(C) == 0, roots, pltpu.roll(roots, HALF, 1))


def times(ref, value):
    return jnp.dot(ref[...], value.astype(BF), preferred_element_type=F32)


def own_products(near_ref, far_ref, front, turned):
    left = left_half(front.shape)
    zero = jnp.zeros_like(front)
    return times(near_ref, jnp.where(left, front, zero)) + times(far_ref, jnp.where(left, zero, turned))


def other_products(near_ref, far_ref, front, turned):
    left = left_half(front.shape)
    zero = jnp.zeros_like(front)
    return times(near_ref, jnp.where(left, zero, front)) + times(far_ref, jnp.where(left, turned, zero))


def first_values(row_block, roots_ref, values_ref, hop_ref, kept_ref):
    core, pair = lax.axis_index(C), lax.axis_index(Z) * 2 * PV
    base_own, base_other = pair + core * PV, pair + (1 - core) * PV
    roots = own_roots(roots_ref)
    turned = pltpu.roll(roots, HALF, 1)
    row = lax.broadcasted_iota(jnp.int32, values_ref.shape[1:], 0)
    vertex = (row // PV) * row_block + row % PV + base_own
    values_ref[0] = (vertex == roots).astype(F32).astype(BF)
    values_ref[1] = (vertex == turned).astype(F32).astype(BF)
    state = hop_ref.shape
    left = left_half(state)
    vertex = lax.broadcasted_iota(jnp.int32, state, 0) + lax.axis_index(ROW) * row_block
    is_root = vertex + jnp.where(left, base_own, base_other) == jnp.where(left, roots, turned)
    kept_ref[...] = is_root.astype(F32)
    hop_ref[...] = jnp.where(is_root, 0, LEVELS + 1)


def first_products(values_ref, near_ref, far_ref, mine_ref, theirs_ref):
    near, far = times(near_ref, values_ref[0]), times(far_ref, values_ref[1])
    left = left_half(near.shape)
    mine_ref[...] = jnp.where(left, near, far).astype(BF)
    theirs_ref[...] = jnp.where(left, far, near).astype(BF)


def add_kernel(mine_ref, both_ref, sent_ref):
    sent_ref[...] = (mine_ref[...].astype(F32) + both_ref[1 - lax.axis_index(C)].astype(F32)).astype(BF)


def level_kernel(front_ref, own_near, own_far, other_near, other_far, sent_ref):
    front = front_ref[...].astype(F32)
    turned = pltpu.roll(front, HALF, 1)
    total = own_products(own_near, own_far, front, turned)
    total += other_products(other_near, other_far, front, turned)
    sent_ref[...] = total.astype(BF)


def turn_kernel(front_ref, turned_ref):
    turned_ref[...] = pltpu.roll(front_ref[...].astype(F32), HALF, 1).astype(BF)


def turned_kernel(front_ref, turned_ref, own_near, own_far, other_near, other_far, sent_ref):
    front, turned = front_ref[...].astype(F32), turned_ref[...].astype(F32)
    total = own_products(own_near, own_far, front, turned)
    total += other_products(other_near, other_far, front, turned)
    sent_ref[...] = total.astype(BF)


def found(level, parts_ref, hop_ref, kept_ref):
    arrived = parts_ref[0].astype(F32)
    for peer in range(1, parts_ref.shape[0]):
        arrived += parts_ref[peer].astype(F32)
    hop = hop_ref[...]
    newly = (arrived > 0) & (hop == LEVELS + 1)
    path = jnp.where(newly, arrived, 0.0)
    return jnp.where(newly, level, hop), kept_ref[...] + path, path


def update_kernel(level, parts_ref, hop_in, kept_in, hop_ref, kept_ref, front_ref):
    hop_ref[...], kept_ref[...], path = found(level, parts_ref, hop_in, kept_in)
    path = path.astype(BF)
    for peer in range(front_ref.shape[0]):
        front_ref[peer] = path


def last_kernel(parts_ref, hop_in, kept_in, mine_ref, theirs_ref, sums_ref):
    hop, kept, _ = found(LEVELS, parts_ref, hop_in, kept_in)
    hops = hop.astype(F32)
    left = left_half(hop.shape)
    mine_ref[...] = jnp.where(left, hops, pltpu.roll(kept, HALF, 1))
    theirs_ref[...] = jnp.where(left, pltpu.roll(hops, HALF, 1), kept)
    sums = []
    for level in range(1, LEVELS + 1):
        at = hop == level
        count = jnp.sum(at.astype(F32), axis=0, keepdims=True)
        total = jnp.sum(jnp.where(at, kept, 0.0), axis=0, keepdims=True)
        count, total = count + pltpu.roll(count, HALF, 1), total + pltpu.roll(total, HALF, 1)
        sums.append(jnp.where(left_half(count.shape), count, total))
    sums = jnp.concatenate(sums, axis=0)
    for peer in range(sums_ref.shape[0]):
        sums_ref[peer] = sums


def sum_kernel(parts_ref, sums_ref):
    sums = jnp.sum(parts_ref[...], axis=0)
    for peer in range(sums_ref.shape[0]):
        sums_ref[peer] = sums


def end_kernel(sums_ref, mine_ref, theirs_ref, hop_ref, share_ref, counts_ref):
    parts = sums_ref[...]
    sums = jnp.sum(parts.reshape(parts.shape[0] // 2, 2, *parts.shape[1:]), axis=0)
    first, second = sums[0], sums[1]
    left = left_half(first.shape)
    counts = jnp.where(left, first, pltpu.roll(second, HALF, 1))
    totals = jnp.where(left, pltpu.roll(first, HALF, 1), second)
    counts_ref[...] = counts
    factor = counts / jnp.maximum(totals, 1.0)
    mine, theirs = mine_ref[...], theirs_ref[...]
    is_first = lax.axis_index(C) == 0
    low, high = jnp.where(is_first, mine, theirs), jnp.where(is_first, theirs, mine)
    left = left_half(low.shape)
    hop = jnp.where(left, low, pltpu.roll(high, HALF, 1)).astype(jnp.int32)
    kept = jnp.where(left, pltpu.roll(low, HALF, 1), high)
    scale = jnp.where(hop == 0, 1.0, 0.0)
    for level in range(1, LEVELS + 1):
        scale = jnp.where(hop == level, factor[level - 1 : level], scale)
    hop_ref[...] = hop
    share_ref[...] = kept * scale


def exchanged(value, axis):
    return lax.all_to_all(value, axis, 0, 0, tiled=True)


def local(tile_weights, tile_pos, tile_total, root_ids):
    rows_all, z_all = lax.axis_size(ROW), lax.axis_size(Z)
    row_block, sources, dests = z_all * 2 * PV, rows_all * PV, z_all * PV
    bf = lambda *shape: jax.ShapeDtypeStruct(shape, BF)
    f32 = lambda *shape: jax.ShapeDtypeStruct(shape, F32)
    hops = jax.ShapeDtypeStruct((PV, ROOTS), jnp.int32)
    swap = [(0, 1), (1, 0)]

    slots = tile_weights.shape[2]
    held = lambda value: pltpu.with_memory_space_constraint(value, pltpu.HBM)
    near, far, mine, theirs, hop, kept = call(
        functools.partial(start_kernel, row_block),
        (bf(dests, sources), bf(dests, sources), bf(dests, ROOTS), bf(dests, ROOTS), hops, f32(PV, ROOTS)),
        [SMEM, ANY, ANY, ANY],
        tile_total,
        held(tile_pos[0, 0]),
        held(tile_weights[0, 0]),
        held(root_ids[None]),
        scratch=[
            pltpu.SMEM((2, slots), jnp.int32),
            pltpu.VMEM((slots, TILE, TILE), BF),
            pltpu.VMEM((1, ROOTS), jnp.int32),
            pltpu.VMEM((2, sources, ROOTS), BF),
            pltpu.SemaphoreType.DMA,
            pltpu.SemaphoreType.DMA,
            pltpu.SemaphoreType.DMA((CHUNKS,)),
        ],
    )
    both = lax.all_gather(theirs, C)
    blocks = (near, far, lax.ppermute(near, C, swap), lax.ppermute(far, C, swap))
    sent = call(add_kernel, bf(dests, ROOTS), [VMEM] * 2, mine, both)
    for level in range(1, LEVELS):
        parts = exchanged(sent.reshape(z_all, PV, ROOTS), Z)
        hop, kept, front = call(
            functools.partial(update_kernel, level),
            (hops, f32(PV, ROOTS), bf(rows_all, PV, ROOTS)),
            [VMEM] * 3,
            parts,
            hop,
            kept,
        )
        front = exchanged(front, ROW).reshape(sources, ROOTS)
        if level == 1:
            turned = call(turn_kernel, bf(sources, ROOTS), [VMEM], front)
            sent = call(turned_kernel, bf(dests, ROOTS), [VMEM] * 6, front, turned, *blocks)
        else:
            sent = call(level_kernel, bf(dests, ROOTS), [VMEM] * 5, front, *blocks)
    parts = exchanged(sent.reshape(z_all, PV, ROOTS), Z)
    mine, theirs, sums = call(
        last_kernel,
        (f32(PV, ROOTS), f32(PV, ROOTS), f32(z_all, LEVELS, ROOTS)),
        [VMEM] * 3,
        parts,
        hop,
        kept,
    )
    theirs = lax.ppermute(theirs, C, swap)
    sums, theirs = lax.optimization_barrier((exchanged(sums, Z), theirs))
    sums = call(sum_kernel, f32(2 * rows_all, LEVELS, ROOTS), [VMEM], sums)
    sums = exchanged(sums, (Y, X, C))
    return call(end_kernel, (hops, f32(PV, ROOTS), f32(LEVELS, ROOTS)), [VMEM] * 3, sums, mine, theirs)


def solution(mesh):
    torus = Mesh(mesh.devices.reshape(4, 4, 16, 2), (Y, X, Z, C))
    return jax.shard_map(
        local,
        mesh=torus,
        in_specs=(P(ROW, COL, None, None, None), P(ROW, COL, None, None), P(ROW, COL), P()),
        out_specs=(P((Y, X, Z, C), None), P((Y, X, Z, C), None), P()),
        check_vma=False,
    )
```

```python
import functools

import jax
import jax.numpy as jnp
from jax import lax
from jax.experimental import pallas as pl
from jax.experimental.pallas import tpu as pltpu
from jax.sharding import Mesh
from jax.sharding import PartitionSpec as P

ROOTS = 128
HALF = ROOTS // 2
PV = 32
LEVELS = 4
TILE = 128
GRANT = 8 << 20
CHUNKS = 4
Y, X, Z, C = "y", "x", "z", "c"
ROW = (Y, X)
COL = (Z, C)
VMEM = pl.BlockSpec(memory_space=pltpu.VMEM)
SMEM = pl.BlockSpec(memory_space=pltpu.SMEM)
ANY = pl.BlockSpec(memory_space=pl.ANY)
BF = jnp.bfloat16
F32 = jnp.float32


def call(kernel, out_shape, in_specs, *operands, scratch=()):
    return pl.pallas_call(
        kernel,
        out_shape=out_shape,
        in_specs=in_specs,
        out_specs=jax.tree.map(lambda _: VMEM, out_shape),
        scratch_shapes=scratch,
        compiler_params=pltpu.CompilerParams(vmem_limit_bytes=GRANT),
    )(*operands)


def start_kernel(
    row_block,
    total_ref,
    pos_hbm,
    tiles_hbm,
    roots_hbm,
    near_ref,
    far_ref,
    mine_ref,
    theirs_ref,
    hop_ref,
    kept_ref,
    pos_ref,
    tiles_ref,
    roots_ref,
    values_ref,
    pos_sem,
    roots_sem,
    tile_sems,
):
    core = lax.axis_index(C)
    slots = tiles_ref.shape[0]
    step = slots // CHUNKS
    pos_copy = pltpu.make_async_copy(pos_hbm, pos_ref, pos_sem)
    pos_copy.start()
    roots_copy = pltpu.make_async_copy(roots_hbm, roots_ref, roots_sem)
    roots_copy.start()
    tile_copies = []
    for chunk in range(CHUNKS):
        part = pl.ds(chunk * step, step)
        tile_copies.append(pltpu.make_async_copy(tiles_hbm.at[part], tiles_ref.at[part], tile_sems.at[chunk]))
    total = total_ref[0, 0]
    for chunk in reversed(range(CHUNKS)):
        pl.when(chunk * step < total)(tile_copies[chunk].start)
    for block_ref in (near_ref, far_ref):
        block_ref[...] = jnp.zeros_like(block_ref)

    roots_copy.wait()
    first_values(row_block, roots_ref, values_ref, hop_ref, kept_ref)
    pos_copy.wait()
    row_tiles, column_tiles = near_ref.shape[0] // (2 * PV), near_ref.shape[1] // TILE
    def place(chunk):
        tile_copies[chunk].wait()
        for slot in reversed(range(chunk * step, (chunk + 1) * step)):
            dest = jnp.minimum(pos_ref[0, slot], row_tiles - 1)
            source = jnp.minimum(pos_ref[1, slot], column_tiles - 1)
            lanes = pl.ds(pl.multiple_of(source * TILE, TILE), TILE)
            used = slot < total
            for part in range(2):
                for half, block_ref in enumerate((near_ref, far_ref)):
                    first = pl.multiple_of(part * 2 * PV + (half ^ core) * PV, PV)
                    rows = pl.multiple_of(dest * 2 * PV + part * PV, PV)
                    tile = tiles_ref[slot, pl.ds(first, PV), :]
                    block_ref[pl.ds(rows, PV), lanes] = jnp.where(used, tile, jnp.zeros_like(tile))

    for chunk in reversed(range(CHUNKS)):
        pl.when(chunk * step < total)(functools.partial(place, chunk))

    first_products(values_ref, near_ref, far_ref, mine_ref, theirs_ref)


def left_half(shape):
    return lax.broadcasted_iota(jnp.int32, shape, len(shape) - 1) < HALF


def own_roots(roots_ref):
    roots = roots_ref[...]
    return jnp.where(lax.axis_index(C) == 0, roots, pltpu.roll(roots, HALF, 1))


def times(ref, value):
    return jnp.dot(ref[...], value.astype(BF), preferred_element_type=F32)


def own_products(near_ref, far_ref, front, turned):
    left = left_half(front.shape)
    zero = jnp.zeros_like(front)
    return times(near_ref, jnp.where(left, front, zero)) + times(far_ref, jnp.where(left, zero, turned))


def other_products(near_ref, far_ref, front, turned):
    left = left_half(front.shape)
    zero = jnp.zeros_like(front)
    return times(near_ref, jnp.where(left, zero, front)) + times(far_ref, jnp.where(left, turned, zero))


def first_values(row_block, roots_ref, values_ref, hop_ref, kept_ref):
    core, pair = lax.axis_index(C), lax.axis_index(Z) * 2 * PV
    base_own, base_other = pair + core * PV, pair + (1 - core) * PV
    roots = own_roots(roots_ref)
    turned = pltpu.roll(roots, HALF, 1)
    row = lax.broadcasted_iota(jnp.int32, values_ref.shape[1:], 0)
    vertex = (row // PV) * row_block + row % PV + base_own
    values_ref[0] = (vertex == roots).astype(F32).astype(BF)
    values_ref[1] = (vertex == turned).astype(F32).astype(BF)
    state = hop_ref.shape
    left = left_half(state)
    vertex = lax.broadcasted_iota(jnp.int32, state, 0) + lax.axis_index(ROW) * row_block
    is_root = vertex + jnp.where(left, base_own, base_other) == jnp.where(left, roots, turned)
    kept_ref[...] = is_root.astype(F32)
    hop_ref[...] = jnp.where(is_root, 0, LEVELS + 1)


def first_products(values_ref, near_ref, far_ref, mine_ref, theirs_ref):
    near, far = times(near_ref, values_ref[0]), times(far_ref, values_ref[1])
    left = left_half(near.shape)
    mine_ref[...] = jnp.where(left, near, far).astype(BF)
    theirs_ref[...] = jnp.where(left, far, near).astype(BF)


def add_kernel(mine_ref, both_ref, sent_ref):
    sent_ref[...] = (mine_ref[...].astype(F32) + both_ref[1 - lax.axis_index(C)].astype(F32)).astype(BF)


def level_kernel(front_ref, own_near, own_far, other_near, other_far, sent_ref):
    front = front_ref[...].astype(F32)
    turned = pltpu.roll(front, HALF, 1)
    total = own_products(own_near, own_far, front, turned)
    total += other_products(other_near, other_far, front, turned)
    sent_ref[...] = total.astype(BF)


def turn_kernel(front_ref, turned_ref):
    turned_ref[...] = pltpu.roll(front_ref[...].astype(F32), HALF, 1).astype(BF)


def turned_kernel(front_ref, turned_ref, own_near, own_far, other_near, other_far, sent_ref):
    front, turned = front_ref[...].astype(F32), turned_ref[...].astype(F32)
    total = own_products(own_near, own_far, front, turned)
    total += other_products(other_near, other_far, front, turned)
    sent_ref[...] = total.astype(BF)


def found(level, parts_ref, hop_ref, kept_ref):
    arrived = parts_ref[0].astype(F32)
    for peer in range(1, parts_ref.shape[0]):
        arrived += parts_ref[peer].astype(F32)
    hop = hop_ref[...]
    newly = (arrived > 0) & (hop == LEVELS + 1)
    path = jnp.where(newly, arrived, 0.0)
    return jnp.where(newly, level, hop), kept_ref[...] + path, path


def update_kernel(level, parts_ref, hop_in, kept_in, hop_ref, kept_ref, front_ref):
    hop_ref[...], kept_ref[...], path = found(level, parts_ref, hop_in, kept_in)
    path = path.astype(BF)
    for peer in range(front_ref.shape[0]):
        front_ref[peer] = path


def last_kernel(parts_ref, hop_in, kept_in, mine_ref, theirs_ref, sums_ref):
    hop, kept, _ = found(LEVELS, parts_ref, hop_in, kept_in)
    hops = hop.astype(F32)
    left = left_half(hop.shape)
    mine_ref[...] = jnp.where(left, hops, pltpu.roll(kept, HALF, 1))
    theirs_ref[...] = jnp.where(left, pltpu.roll(hops, HALF, 1), kept)
    sums = []
    for level in range(1, LEVELS + 1):
        at = hop == level
        count = jnp.sum(at.astype(F32), axis=0, keepdims=True)
        total = jnp.sum(jnp.where(at, kept, 0.0), axis=0, keepdims=True)
        count, total = count + pltpu.roll(count, HALF, 1), total + pltpu.roll(total, HALF, 1)
        sums.append(jnp.where(left_half(count.shape), count, total))
    sums = jnp.concatenate(sums, axis=0)
    for peer in range(sums_ref.shape[0]):
        sums_ref[peer] = sums


def sum_kernel(parts_ref, sums_ref):
    sums = jnp.sum(parts_ref[...], axis=0)
    for peer in range(sums_ref.shape[0]):
        sums_ref[peer] = sums


def end_kernel(sums_ref, mine_ref, theirs_ref, hop_ref, share_ref, counts_ref):
    parts = sums_ref[...]
    sums = jnp.sum(parts.reshape(parts.shape[0] // 2, 2, *parts.shape[1:]), axis=0)
    first, second = sums[0], sums[1]
    left = left_half(first.shape)
    counts = jnp.where(left, first, pltpu.roll(second, HALF, 1))
    totals = jnp.where(left, pltpu.roll(first, HALF, 1), second)
    counts_ref[...] = counts
    factor = counts / jnp.maximum(totals, 1.0)
    mine, theirs = mine_ref[...], theirs_ref[...]
    is_first = lax.axis_index(C) == 0
    low, high = jnp.where(is_first, mine, theirs), jnp.where(is_first, theirs, mine)
    left = left_half(low.shape)
    hop = jnp.where(left, low, pltpu.roll(high, HALF, 1)).astype(jnp.int32)
    kept = jnp.where(left, pltpu.roll(low, HALF, 1), high)
    scale = jnp.where(hop == 0, 1.0, 0.0)
    for level in range(1, LEVELS + 1):
        scale = jnp.where(hop == level, factor[level - 1 : level], scale)
    hop_ref[...] = hop
    share_ref[...] = kept * scale


def exchanged(value, axis):
    return lax.all_to_all(value, axis, 0, 0, tiled=True)


def local(tile_weights, tile_pos, tile_total, root_ids):
    rows_all, z_all = lax.axis_size(ROW), lax.axis_size(Z)
    row_block, sources, dests = z_all * 2 * PV, rows_all * PV, z_all * PV
    bf = lambda *shape: jax.ShapeDtypeStruct(shape, BF)
    f32 = lambda *shape: jax.ShapeDtypeStruct(shape, F32)
    hops = jax.ShapeDtypeStruct((PV, ROOTS), jnp.int32)
    swap = [(0, 1), (1, 0)]

    slots = tile_weights.shape[2]
    held = lambda value: pltpu.with_memory_space_constraint(value, pltpu.HBM)
    near, far, mine, theirs, hop, kept = call(
        functools.partial(start_kernel, row_block),
        (bf(dests, sources), bf(dests, sources), bf(dests, ROOTS), bf(dests, ROOTS), hops, f32(PV, ROOTS)),
        [SMEM, ANY, ANY, ANY],
        tile_total,
        held(tile_pos[0, 0]),
        held(tile_weights[0, 0]),
        held(root_ids[None]),
        scratch=[
            pltpu.SMEM((2, slots), jnp.int32),
            pltpu.VMEM((slots, TILE, TILE), BF),
            pltpu.VMEM((1, ROOTS), jnp.int32),
            pltpu.VMEM((2, sources, ROOTS), BF),
            pltpu.SemaphoreType.DMA,
            pltpu.SemaphoreType.DMA,
            pltpu.SemaphoreType.DMA((CHUNKS,)),
        ],
    )
    both = lax.all_gather(theirs, C)
    blocks = (near, far, lax.ppermute(near, C, swap), lax.ppermute(far, C, swap))
    sent = call(add_kernel, bf(dests, ROOTS), [VMEM] * 2, mine, both)
    for level in range(1, LEVELS):
        parts = exchanged(sent.reshape(z_all, PV, ROOTS), Z)
        hop, kept, front = call(
            functools.partial(update_kernel, level),
            (hops, f32(PV, ROOTS), bf(rows_all, PV, ROOTS)),
            [VMEM] * 3,
            parts,
            hop,
            kept,
        )
        front = exchanged(front, ROW).reshape(sources, ROOTS)
        if level == 1:
            turned = call(turn_kernel, bf(sources, ROOTS), [VMEM], front)
            sent = call(turned_kernel, bf(dests, ROOTS), [VMEM] * 6, front, turned, *blocks)
        else:
            sent = call(level_kernel, bf(dests, ROOTS), [VMEM] * 5, front, *blocks)
    parts = exchanged(sent.reshape(z_all, PV, ROOTS), Z)
    mine, theirs, sums = call(
        last_kernel,
        (f32(PV, ROOTS), f32(PV, ROOTS), f32(z_all, LEVELS, ROOTS)),
        [VMEM] * 3,
        parts,
        hop,
        kept,
    )
    theirs = lax.ppermute(theirs, C, swap)
    sums, theirs = lax.optimization_barrier((exchanged(sums, Z), theirs))
    sums = call(sum_kernel, f32(2 * rows_all, LEVELS, ROOTS), [VMEM], sums)
    sums = exchanged(sums, (Y, X, C))
    return call(end_kernel, (hops, f32(PV, ROOTS), f32(LEVELS, ROOTS)), [VMEM] * 3, sums, mine, theirs)


def solution(mesh):
    torus = Mesh(mesh.devices.reshape(4, 4, 16, 2), (Y, X, Z, C))
    return jax.shard_map(
        local,
        mesh=torus,
        in_specs=(P(ROW, COL, None, None, None), P(ROW, COL, None, None), P(ROW, COL), P()),
        out_specs=(P((Y, X, Z, C), None), P((Y, X, Z, C), None), P()),
        check_vma=False,
    )
```
